128 devices in a mesh: dp: 16 (over x, z), seq: 8 (over y, core).
Axes of the slice: x: 4, y: 4, z: 4, core: 2. Of those that a mesh axis runs over, the one named last changes fastest.
Arguments:
- tokens: bfloat16 [16384, 7168], P(('dp', 'seq')), may hold values from -6 to 6
- cotangent: bfloat16 [16384, 7168], P(('dp', 'seq')), may hold values from -0.29882812 to 0.29882812
- chosen_expert_index: int32 [16384, 1], P(('dp', 'seq')), may hold values from 0 to 15; in each aligned block of 128 rows (0 to 127, 128 to 255, ...) at most 10 rows name the same one
- router_weight: float32 [16384, 1], P(('dp', 'seq')), may hold values from 0.2 to 1
- frozen_gate_weight: bfloat16 [16, 7168, 2048], P('dp', None, 'seq'), may hold values from -0.0625 to 0.0625
- frozen_up_weight: bfloat16 [16, 7168, 2048], P('dp', None, 'seq'), may hold values from -0.0625 to 0.0625
- frozen_down_weight: bfloat16 [16, 2048, 7168], P('dp', 'seq'), may hold values from -0.125 to 0.125
- gate_adapter_first: bfloat16 [16, 16, 7168], P('dp'), may hold values from -0.0625 to 0.0625
- gate_adapter_second: bfloat16 [16, 16, 2048], P('dp', None, 'seq'), may hold values from -1.5 to 1.5
- down_adapter_first: bfloat16 [16, 16, 2048], P('dp', None, 'seq'), may hold values from -0.125 to 0.125
- down_adapter_second: bfloat16 [16, 16, 7168], P('dp'), may hold values from -1.5 to 1.5
Outputs:
- grad_gate_a: float32 [16, 16, 7168], P('dp', None, 'seq')
- grad_gate_b: float32 [16, 16, 2048], P('dp', None, 'seq')
- grad_down_a: float32 [16, 16, 2048], P('dp', None, 'seq')
- grad_down_b: float32 [16, 16, 7168], P('dp', None, 'seq')
The draws below stay inside these ranges and needn't reach their ends.
Inputs may be any that keep to these rules, and one draw needn't show every extreme that they name: `chosen_expert_index`: among the entries of the rows of one device (tokens b * 128 to (b + 1) * 128 - 1) no expert is named more than 10 times, and in some device's rows one expert is named exactly 10 times.
All inputs are finite; a program needn't handle non-finite values.
Results may differ from the reference program's by a relative error of at most 0.007.
Values may be sent and summed in bfloat16 or wider, within the bound.
No kernel may reach another device: no remote copies, remote signals or barrier semaphores. Data moves between devices by JAX's collectives and lax.ppermute only.
A program may use at most 256 MiB of HBM per device.

```python
import math
import jax
import jax.numpy as jnp
import numpy as np
from jax import lax

MODEL_WIDTH = 7168
HIDDEN_UNITS = 2048
ADAPTER_RANK = 16
TOP = 1
TOK_DEV = 128
EXPERT_COUNT = 16
CAP = 10
TOKENS = 16384


def steps_of(rng, dims, shards, smallest, top_value):
    loudness = 1.0
    for dim, shards_of in shards:
        heights = jax.random.uniform(jax.random.fold_in(jax.random.fold_in(rng, 6), dim), (shards_of,), jnp.float32, smallest / len(shards), top_value / len(shards))
        loudness = loudness * jnp.repeat(jnp.exp(heights), dims[dim] // shards_of).reshape((-1,) + (1,) * (len(dims) - 1 - dim))
    return loudness


def shared_out(stream_key, own, number, rows, count, top, reach, lean):
    ranking = jax.random.permutation(stream_key, count)
    crowded, ordinary = load_shares(count, rows * top, reach, lean, True), load_shares(count, rows * top, reach, lean, False)
    places = jnp.arange(count)

    def named(tallies, turn):
        used = int((tallies > 0).sum())
        fixed = max(1, used // 4)
        moved = fixed + (places - fixed + turn * (used - fixed)) % max(1, count - fixed)
        return jnp.zeros((count,), jnp.int32).at[ranking[jnp.where(places < fixed, places, moved)]].set(jnp.asarray(tallies, jnp.int32))

    tallies = jnp.where(number % 4 == 0, named(crowded, number // 4), named(ordinary, number - number // 4 - 1))
    mixed = jax.random.permutation(jax.random.fold_in(own, 3), count)
    donor, sink = mixed[0:count // 2 * 2:2], mixed[1:count // 2 * 2:2]
    room = jnp.minimum(tallies[donor] - 1, reach - tallies[sink]) // 2
    room = jnp.where((donor == ranking[0]) | (sink == ranking[0]) | (tallies[sink] == 0), 0, jnp.maximum(room, 0))
    moved = jax.random.randint(jax.random.fold_in(own, 4), (count // 2,), 0, 1 << 20) % (room + 1)
    tallies = tallies.at[donor].add(-moved).at[sink].add(moved)
    labels = jnp.searchsorted(jnp.cumsum(tallies), jnp.arange(rows * top), side="right").astype(jnp.int32)
    grid = labels.reshape(top, rows).T
    grid = grid[jax.random.permutation(jax.random.fold_in(own, 1), rows)]
    turn = jax.random.randint(jax.random.fold_in(own, 2), (rows, 1), 0, top)
    return jnp.take_along_axis(grid, (jnp.arange(top)[None, :] + turn) % top, axis=1)


def load_shares(number_of, total, reach, lean, full):
    loads = [(1 << 20) // math.isqrt(grade ** lean) + 1 for grade in range(1, number_of + 1)]
    largest = reach if full else min(reach, max(-(-total // number_of), total * loads[0] // sum(loads)))
    least = 1 if total - largest >= number_of - 1 else 0
    given, surplus = [largest] + [least] * (number_of - 1), total - largest - least * (number_of - 1)
    while surplus > 0:
        movable = [i for i in range(1, number_of) if given[i] < largest] or [i for i in range(1, number_of) if given[i] < reach]
        mass, left = sum([loads[i] for i in movable]), surplus
        for i in movable:
            addition = min(reach - given[i], max(1, left * loads[i] // mass), surplus)
            given[i] = given[i] + addition
            surplus = surplus - addition
    return np.array(given)


def bell_draw(stream_key, extent, spread, limit, pieces=(), kind=jnp.bfloat16):
    values = jax.random.normal(stream_key, extent, jnp.float32) * spread
    if len(pieces) > 0:
        values = steps_of(stream_key, extent, pieces, -0.22, 0.18) * values
    return jnp.clip(values, min=-limit, max=limit).astype(kind)


def setup_inputs(seed: int = 0) -> dict:
    streams_of = jax.random.split(jax.random.key(seed), 12)
    tokens = bell_draw(streams_of[0], (TOKENS, MODEL_WIDTH), 1.0, 6.0, ((0, 128),))
    cotangent = bell_draw(streams_of[1], (TOKENS, MODEL_WIDTH), 0.05, 0.29882812, ((0, 128),))
    chosen_expert_index_keys = jax.random.split(jax.random.fold_in(streams_of[2], 1), TOKENS // TOK_DEV)
    chosen_expert_index_turns = jax.random.permutation(jax.random.fold_in(streams_of[2], 3), TOKENS // TOK_DEV)
    chosen_expert_index = jax.vmap(lambda own, number: shared_out(jax.random.fold_in(streams_of[2], 2), own, number, TOK_DEV, EXPERT_COUNT, TOP, CAP, 1))(chosen_expert_index_keys, chosen_expert_index_turns).reshape((TOKENS, TOP))
    router_weight = jnp.clip(jnp.exp(math.log(1.0) - 1.609438 * jax.random.uniform(streams_of[3], (TOKENS, TOP), jnp.float32) ** steps_of(streams_of[3], (TOKENS, TOP), ((0, 128),), -0.2, 0.2)), 0.2, 1.0)
    frozen_gate_weight = bell_draw(streams_of[4], (EXPERT_COUNT, MODEL_WIDTH, HIDDEN_UNITS), MODEL_WIDTH ** -0.5, 0.0625, ((0, 16), (2, 8)))
    frozen_up_weight = bell_draw(streams_of[5], (EXPERT_COUNT, MODEL_WIDTH, HIDDEN_UNITS), MODEL_WIDTH ** -0.5, 0.0625, ((0, 16), (2, 8)))
    frozen_down_weight = bell_draw(streams_of[6], (EXPERT_COUNT, HIDDEN_UNITS, MODEL_WIDTH), HIDDEN_UNITS ** -0.5, 0.125, ((0, 16), (1, 8)))
    gate_adapter_first = bell_draw(streams_of[7], (EXPERT_COUNT, ADAPTER_RANK, MODEL_WIDTH), MODEL_WIDTH ** -0.5, 0.0625, ((0, 16),))
    gate_adapter_second = bell_draw(streams_of[8], (EXPERT_COUNT, ADAPTER_RANK, HIDDEN_UNITS), ADAPTER_RANK ** -0.5, 1.5, ((0, 16), (2, 8)))
    down_adapter_first = bell_draw(streams_of[9], (EXPERT_COUNT, ADAPTER_RANK, HIDDEN_UNITS), HIDDEN_UNITS ** -0.5, 0.125, ((0, 16), (2, 8)))
    down_adapter_second = bell_draw(streams_of[10], (EXPERT_COUNT, ADAPTER_RANK, MODEL_WIDTH), ADAPTER_RANK ** -0.5, 1.5, ((0, 16),))
    return dict(tokens=tokens, cotangent=cotangent, chosen_expert_index=chosen_expert_index, router_weight=router_weight, frozen_gate_weight=frozen_gate_weight, frozen_up_weight=frozen_up_weight, frozen_down_weight=frozen_down_weight, gate_adapter_first=gate_adapter_first, gate_adapter_second=gate_adapter_second, down_adapter_first=down_adapter_first, down_adapter_second=down_adapter_second)


def contract_last(left, right):
    return lax.dot_general(left.astype(jnp.float32), right.astype(jnp.float32), (((1,), (1,)), ((), ())))


def contract_first(left, right):
    return lax.dot_general(left.astype(jnp.float32), right.astype(jnp.float32), (((0,), (0,)), ((), ())))


def expert_terms(rows_in, rows_back, gate_w, up_w, down_w, gate_a, gate_b, down_a, down_b):
    lowrank_in = contract_last(rows_in, gate_a).astype(jnp.bfloat16)
    gate_pre = jnp.dot(rows_in, gate_w, preferred_element_type=jnp.float32) + jnp.dot(lowrank_in, gate_b, preferred_element_type=jnp.float32)
    up_pre = jnp.dot(rows_in, up_w, preferred_element_type=jnp.float32)
    sigmoid_val = jax.nn.sigmoid(gate_pre)
    hidden = (gate_pre * sigmoid_val * up_pre).astype(jnp.bfloat16)
    lowrank_back = contract_last(rows_back, down_b).astype(jnp.bfloat16)
    hidden_grad = contract_last(rows_back, down_w) + jnp.dot(lowrank_back, down_a, preferred_element_type=jnp.float32)
    gate_grad = (hidden_grad * up_pre * sigmoid_val * (1.0 + gate_pre * (1.0 - sigmoid_val))).astype(jnp.bfloat16)
    grad_gb = contract_first(lowrank_in, gate_grad)
    gate_back = contract_last(gate_grad, gate_b)
    grad_ga = contract_first(gate_back, rows_in)
    grad_da = contract_first(lowrank_back, hidden)
    down_low = contract_last(hidden, down_a)
    grad_db = contract_first(down_low, rows_back)
    return grad_ga, grad_gb, grad_da, grad_db


def reference(tokens, cotangent, chosen_expert_index, router_weight, frozen_gate_weight, frozen_up_weight, frozen_down_weight, gate_adapter_first, gate_adapter_second, down_adapter_first, down_adapter_second):
    blocks = TOKENS // TOK_DEV
    entries = TOK_DEV * TOP
    flat_ids = chosen_expert_index.reshape(blocks, entries).astype(jnp.int32)
    onehot = (flat_ids[:, :, None] == jnp.arange(EXPERT_COUNT, dtype=jnp.int32)[None, None, :]).astype(jnp.int32)
    earlier = (jnp.cumsum(onehot, axis=1) - onehot).astype(jnp.int32)
    slot = jnp.sum(earlier * onehot, axis=2).astype(jnp.int32)
    position = (jnp.arange(blocks, dtype=jnp.int32)[:, None] * CAP + slot).reshape(-1).astype(jnp.int32)
    owner = flat_ids.reshape(-1)
    rows_in = jnp.broadcast_to(tokens[:, None, :], (TOKENS, TOP, MODEL_WIDTH)).reshape(-1, MODEL_WIDTH)
    scaled = (cotangent.astype(jnp.float32)[:, None, :] * router_weight[:, :, None]).astype(jnp.bfloat16).reshape(-1, MODEL_WIDTH)
    incoming_buffer = jnp.zeros((EXPERT_COUNT, blocks * CAP, MODEL_WIDTH), jnp.bfloat16).at[owner, position].set(rows_in)
    return_buffer = jnp.zeros((EXPERT_COUNT, blocks * CAP, MODEL_WIDTH), jnp.bfloat16).at[owner, position].set(scaled)

    def single_expert(items):
        return expert_terms(*items)

    adapter_gradients = lax.map(single_expert, (incoming_buffer, return_buffer, frozen_gate_weight, frozen_up_weight, frozen_down_weight, gate_adapter_first, gate_adapter_second, down_adapter_first, down_adapter_second))
    return adapter_gradients[0], adapter_gradients[1], adapter_gradients[2], adapter_gradients[3]
```

```python
import jax
import jax.numpy as jnp
from jax import lax
from jax.sharding import PartitionSpec as P

PIECES = 4


def contract_last(left, right):
    return lax.dot_general(
        left, right, (((1,), (1,)), ((), ())), preferred_element_type=jnp.float32
    )


def contract_first(left, right):
    return lax.dot_general(
        left, right, (((0,), (0,)), ((), ())), preferred_element_type=jnp.float32
    )


def shift_y(value, step):
    size = lax.axis_size("seq")
    planes = size // 2
    pairs = [
        (y * 2 + c, ((y + step) % planes) * 2 + c) for y in range(planes) for c in range(2)
    ]
    return lax.ppermute(value, "seq", pairs)


def swap_core(value):
    size = lax.axis_size("seq")
    return lax.ppermute(value, "seq", [(i, i ^ 1) for i in range(size)])


def gather_y(rows):
    half = rows.shape[0] // 2
    before, after = shift_y(rows, 1), shift_y(rows, -1)
    far_a, far_b = shift_y(before[:half], 1), shift_y(after[half:], -1)
    return jnp.concatenate([rows, before, after, far_a, far_b], axis=0)


def body(
    tokens,
    cotangent,
    chosen_expert_index,
    router_weight,
    frozen_gate_weight,
    frozen_up_weight,
    frozen_down_weight,
    gate_adapter_first,
    gate_adapter_second,
    down_adapter_first,
    down_adapter_second,
):
    experts = lax.axis_size("dp")
    tok_count, top = chosen_expert_index.shape
    width = tokens.shape[1]
    part = width // PIECES
    capacity = 5 * tok_count * top // (4 * experts)
    slots = experts * capacity
    gate_w, up_w, down_w = frozen_gate_weight[0], frozen_up_weight[0], frozen_down_weight[0]
    gate_a, gate_b = gate_adapter_first[0], gate_adapter_second[0]
    down_a, down_b = down_adapter_first[0], down_adapter_second[0]
    weights = (
        (gate_w, up_w, down_w, gate_b, down_a),
        tuple(swap_core(w) for w in (gate_w, up_w, down_w, gate_b, down_a)),
    )

    flat_ids = chosen_expert_index.reshape(-1)
    onehot = (flat_ids[:, None] == jnp.arange(experts, dtype=jnp.int32)[None, :]).astype(jnp.int32)
    earlier = jnp.cumsum(onehot, axis=0) - onehot
    slot = jnp.sum(earlier * onehot, axis=1)
    at_row = jnp.arange(experts * PIECES * capacity, dtype=jnp.int32)
    row_expert = at_row // (PIECES * capacity)
    row_piece = at_row // capacity % PIECES
    row_slot = at_row % capacity
    hit = (row_expert[:, None] == flat_ids[None, :]) & (row_slot[:, None] == slot[None, :])
    placing = jnp.concatenate(
        [(hit & (row_piece == q)[:, None]).astype(jnp.bfloat16) for q in range(PIECES)], axis=1
    )
    at_slot = jnp.arange(slots, dtype=jnp.int32)
    home = (at_slot // capacity) * PIECES * capacity + at_slot % capacity
    taking = [
        ((home + q * capacity)[:, None] == at_row[None, :]).astype(jnp.bfloat16)
        for q in range(PIECES)
    ]

    def route(rows):
        stacked = jnp.concatenate([rows[:, q * part : (q + 1) * part] for q in range(PIECES)], axis=0)
        packed = jnp.dot(placing, stacked, preferred_element_type=jnp.float32).astype(jnp.bfloat16)
        packed = packed.reshape(experts, PIECES * capacity, part)
        got = lax.all_to_all(packed, "dp", split_axis=0, concat_axis=0, tiled=True)
        got = got.reshape(experts * PIECES * capacity, part)
        return jnp.concatenate(
            [
                jnp.dot(take, got, preferred_element_type=jnp.float32).astype(jnp.bfloat16)
                for take in taking
            ],
            axis=1,
        )

    rows_in = gather_y(route(tokens))
    scaled = (cotangent.astype(jnp.float32) * router_weight).astype(jnp.bfloat16)
    rows_back = gather_y(route(scaled))

    lowrank_in = contract_last(rows_in, gate_a).astype(jnp.bfloat16)
    lowrank_back = contract_last(rows_back, down_b).astype(jnp.bfloat16)
    sums, grads = 0.0, []
    for gw, uw, dw, gb, da in weights:
        gate_pre = jnp.dot(rows_in, gw, preferred_element_type=jnp.float32) + jnp.dot(
            lowrank_in, gb, preferred_element_type=jnp.float32
        )
        up_pre = jnp.dot(rows_in, uw, preferred_element_type=jnp.float32)
        sigmoid_val = jax.nn.sigmoid(gate_pre)
        hidden = (gate_pre * sigmoid_val * up_pre).astype(jnp.bfloat16)
        hidden_grad = contract_last(rows_back, dw) + jnp.dot(
            lowrank_back, da, preferred_element_type=jnp.float32
        )
        gate_grad = (
            hidden_grad * up_pre * sigmoid_val * (1.0 + gate_pre * (1.0 - sigmoid_val))
        ).astype(jnp.bfloat16)
        grads.append(
            jnp.stack([contract_first(lowrank_in, gate_grad), contract_first(lowrank_back, hidden)])
        )
        sums = sums + jnp.concatenate([contract_last(gb, gate_grad), contract_last(da, hidden)], axis=0)
    grad_hidden = grads[0] + swap_core(grads[1])

    def in_order(value, order):
        return jnp.concatenate([value[:, i * slots : (i + 1) * slots] for i in order], axis=1)

    sums = (
        sums
        + in_order(shift_y(sums, 1), (2, 0, 3, 1))
        + in_order(shift_y(sums, -1), (1, 3, 0, 2))
        + in_order(shift_y(sums, 2), (3, 2, 1, 0))
    )
    me = lax.axis_index("seq")
    share = width // lax.axis_size("seq")
    rank = gate_a.shape[0]

    def product(first):
        cols_in = lax.dynamic_slice_in_dim(rows_in, first, share, axis=1)
        cols_back = lax.dynamic_slice_in_dim(rows_back, first, share, axis=1)
        return jnp.stack(
            [
                jnp.dot(sums[:rank], cols_in, preferred_element_type=jnp.float32),
                jnp.dot(sums[rank:], cols_back, preferred_element_type=jnp.float32),
            ]
        )

    mine, theirs = product(me * share), product((me ^ 1) * share)
    wide = mine + swap_core(theirs)
    return (wide[:1], grad_hidden[:1], grad_hidden[1:], wide[1:])


def solution(mesh):
    return jax.shard_map(
        body,
        mesh=mesh,
        in_specs=(
            P(("dp", "seq"), None),
            P(("dp", "seq"), None),
            P(("dp", "seq"), None),
            P(("dp", "seq"), None),
            P("dp", None, "seq"),
            P("dp", None, "seq"),
            P("dp", "seq", None),
            P("dp", None, None),
            P("dp", None, "seq"),
            P("dp", None, "seq"),
            P("dp", None, None),
        ),
        out_specs=(
            P("dp", None, "seq"),
            P("dp", None, "seq"),
            P("dp", None, "seq"),
            P("dp", None, "seq"),
        ),
        check_vma=False,
    )
```

```python
import functools

import jax
import jax.numpy as jnp
from jax import lax
from jax.experimental import pallas as pl
from jax.experimental.pallas import tpu as pltpu
from jax.sharding import PartitionSpec as P

PIECES = 4
EARLY = 4
CHUNKS = (2, 2, 3)
DEPTH = 1024
LANES = 128
COVER = 8
MIB = 1 << 20
VMEM_MIB = 56
BF16, F32 = jnp.bfloat16, jnp.float32


def dot(left, right):
    return jnp.dot(left, right, preferred_element_type=F32)


def contract_last(left, right):
    return lax.dot_general(left, right, (((1,), (1,)), ((), ())), preferred_element_type=F32)


def contract_first(left, right):
    return lax.dot_general(left, right, (((0,), (0,)), ((), ())), preferred_element_type=F32)


def shift_y(value, step):
    size = lax.axis_size("seq")
    planes = size // 2
    pairs = [
        (y * 2 + c, ((y + step) % planes) * 2 + c) for y in range(planes) for c in range(2)
    ]
    return lax.ppermute(value, "seq", pairs)


def swap_core(value):
    size = lax.axis_size("seq")
    return lax.ppermute(value, "seq", [(i, i ^ 1) for i in range(size)])


def first_step(rows):
    return shift_y(rows, 1), shift_y(rows, -1)


def split_kernel(before_ref, after_ref, low_ref, high_ref, sems):
    half = low_ref.shape[0]
    low = pltpu.make_async_copy(before_ref.at[pl.ds(0, half)], low_ref, sems.at[0])
    high = pltpu.make_async_copy(after_ref.at[pl.ds(half, half)], high_ref, sems.at[1])
    low.start()
    high.start()
    low.wait()
    high.wait()


def second_step(before, after):
    part = shape((before.shape[0] // 2, before.shape[1]), before.dtype)
    anywhere = pl.BlockSpec(memory_space=pl.ANY)
    low, high = call(
        split_kernel,
        (part, part),
        8,
        moved=2 * before.size * 2,
        in_specs=[anywhere] * 2,
        out_specs=(anywhere,) * 2,
        scratch_shapes=[pltpu.SemaphoreType.DMA((2,))],
    )(before, after)
    return shift_y(low, 1), shift_y(high, -1)


def shape(dims, dtype):
    return jax.ShapeDtypeStruct(dims, dtype)


def call(kernel, outs, mib, flops=0, moved=0, **rest):
    return pl.pallas_call(
        kernel,
        out_shape=outs,
        compiler_params=pltpu.CompilerParams(vmem_limit_bytes=mib * MIB),
        cost_estimate=pl.CostEstimate(flops=COVER * flops, bytes_accessed=COVER * moved, transcendentals=0),
        **rest,
    )


def whole(*dims):
    return pl.BlockSpec(dims, lambda *_: (0,) * len(dims))


def scale_kernel(cot_ref, weight_ref, code_ref, raw_ref, rest_ref):
    count = weight_ref.shape[1]
    column = jnp.broadcast_to(weight_ref[...], (count, count)).T[:, :1]
    early = cot_ref.shape[1] - rest_ref.shape[1]
    for base, size, out in ((0, early, raw_ref), (early, rest_ref.shape[1], rest_ref)):
        for at in range(0, size, 512):
            block = cot_ref[:, base + at : base + at + 512].astype(F32)
            out[:, at : at + 512] = (block * column).astype(BF16)
    codes = jnp.broadcast_to(code_ref[...], (count, count)).astype(F32).T
    raw_ref[:, early:] = codes[:, : raw_ref.shape[1] - early].astype(BF16)


def code_kernel(experts, capacity, ids_ref, code_ref):
    ids = ids_ref[...]
    count = ids.shape[1]
    onehot = (lax.broadcasted_iota(jnp.int32, (experts, count), 0) == ids).astype(F32)
    ahead = (
        lax.broadcasted_iota(jnp.int32, (count, count), 0)
        < lax.broadcasted_iota(jnp.int32, (count, count), 1)
    ).astype(BF16)
    earlier = dot(onehot.astype(BF16), ahead)
    slot = jnp.sum(earlier * onehot, axis=0, keepdims=True).astype(jnp.int32)
    code_ref[...] = ids * capacity + slot


def pack_kernel(spans, code_ref, want_ref, piece_ref, *refs):
    out = refs[-1]
    hit = code_ref[...] == want_ref[...]
    placing = jnp.concatenate(
        [(hit & (piece_ref[...] == q)).astype(BF16) for q in range(PIECES)], axis=1
    )
    at = 0
    for rows, (first, size) in zip(refs, spans):
        part = size // PIECES
        stacked = jnp.concatenate(
            [rows[:, first + q * part : first + (q + 1) * part] for q in range(PIECES)], axis=0
        )
        out[:, at : at + part] = dot(placing, stacked).astype(BF16)
        at += part


def unpack_kernel(got_ref, came_ref, *outs):
    count = got_ref.shape[0]
    take = (
        lax.broadcasted_iota(jnp.int32, (count, count), 1) == came_ref[...]
    ).astype(BF16)
    rows = count // PIECES
    at = 0
    for out in outs:
        part = out.shape[1] // PIECES
        taken = dot(take, got_ref[:, at : at + part]).astype(BF16)
        for q in range(PIECES):
            out[:, q * part : (q + 1) * part] = taken[q * rows : (q + 1) * rows]
        at += part


def pack_raw_kernel(want_ref, plane_ref, *refs):
    pieces, codes, out, placing = refs[:5], refs[5:10], refs[10], refs[11]

    @pl.when(pl.program_id(0) == 0)
    def _():
        code = jnp.concatenate([piece[...] for piece in codes], axis=0).astype(F32)
        count = code.shape[0] // 4
        for k in range(4):
            row = code[k * count : (k + 1) * count].T[:1].astype(jnp.int32)
            hit = (row == want_ref[...]) & (plane_ref[...] == k)
            placing[:, k * count : (k + 1) * count] = hit.astype(BF16)

    stacked = jnp.concatenate([piece[...] for piece in pieces], axis=0)
    out[...] = dot(placing[...], stacked).astype(BF16)


def gate_up_kernel(begins, last, *refs):
    pieces, (gate_o, gate_p, up_o, up_p, first) = refs[:5], refs[5:10]
    refs = refs[10:]
    if not begins:
        prev, refs = refs[:3], refs[3:]
    if last:
        (gb_o, gb_p, da_o, da_p), refs = refs[:4], refs[4:]
        (hidden_ref, factor_ref, low_ref, sums_ref), refs = refs[:4], refs[4:]
    gate, up, low = refs
    step = pl.program_id(0)
    units = gate_o.shape[1]

    @pl.when(step == 0)
    def _():
        for i, total in enumerate((gate, up, low)):
            total[...] = jnp.zeros_like(total) if begins else prev[i][...]

    rows = jnp.concatenate([piece[...] for piece in pieces], axis=0)
    gate[:, :units] += dot(rows, gate_o[...])
    gate[:, units:] += dot(rows, gate_p[...])
    up[:, :units] += dot(rows, up_o[...])
    up[:, units:] += dot(rows, up_p[...])
    low[...] += contract_last(rows, first[...])

    if last:

        @pl.when(step == pl.num_programs(0) - 1)
        def _():
            lowrank_in = low[...].astype(BF16)
            low_ref[...] = lowrank_in
            gate[:, :units] += dot(lowrank_in, gb_o[...])
            gate[:, units:] += dot(lowrank_in, gb_p[...])
            block = 32

            def some(i, carry):
                at = pl.ds(pl.multiple_of(i * block, block), block)
                gate_pre, up_pre = gate[at, :], up[at, :]
                sigmoid_val = jax.nn.sigmoid(gate_pre)
                slope = up_pre * sigmoid_val
                hidden_ref[at, :] = (gate_pre * slope).astype(BF16)
                factor_ref[at, :] = slope * (1.0 + gate_pre * (1.0 - sigmoid_val))
                return carry

            lax.fori_loop(0, gate.shape[0] // block, some, 0)
            sums_ref[...] = contract_last(da_o[...], hidden_ref[:, :units]) + contract_last(
                da_p[...], hidden_ref[:, units:]
            )


def halves(value):
    high = value.astype(BF16)
    return high, (value - high.astype(F32)).astype(BF16)


def order_of(came_ref):
    count = came_ref.shape[0]
    return (lax.broadcasted_iota(jnp.int32, (count, count), 1) == came_ref[...]).astype(BF16)


def raw_kernel(got_ref, came_ref, down_o, down_p, first, total_ref, low_ref, total, low):
    units = down_o.shape[0]
    step = pl.program_id(0)

    @pl.when(step == 0)
    def _():
        total[...] = jnp.zeros_like(total)
        low[...] = jnp.zeros_like(low)

    rows = got_ref[...]
    total[:, :units] += contract_last(rows, down_o[...])
    total[:, units:] += contract_last(rows, down_p[...])
    low[...] += contract_last(rows, first[...])

    @pl.when(step == pl.num_programs(0) - 1)
    def _():
        order = order_of(came_ref)
        for source, out in ((total, total_ref), (low, low_ref)):
            high_part, low_part = halves(source[...])
            out[...] = dot(order, high_part) + dot(order, low_part)


def back_kernel(last, pieces, *refs):
    refs = list(refs)

    def take(number):
        taken = refs[:number]
        del refs[:number]
        return taken

    rows_refs, (down_o, down_p, first) = take(pieces), take(3)
    prev, (factor_ref, hidden_ref, low_in_ref) = take(2), take(3)
    gb_o, gb_p, da_o, da_p = take(4)
    if last:
        sums_before, grads_before, sums_back = take(3)
    sums_ref, grads_ref, total, low = refs
    step = pl.program_id(0)
    units = down_o.shape[0]

    @pl.when(step == 0)
    def _():
        total[...] = prev[0][...]
        low[...] = prev[1][...]

    rows = jnp.concatenate([piece[...] for piece in rows_refs], axis=0)
    total[:, :units] += contract_last(rows, down_o[...])
    total[:, units:] += contract_last(rows, down_p[...])
    low[...] += contract_last(rows, first[...])

    @pl.when(step == pl.num_programs(0) - 1)
    def _():
        lowrank_back = low[...].astype(BF16)
        rank = lowrank_back.shape[1]
        total_o = total[:, :units] + dot(lowrank_back, da_o[...])
        grad_o = (total_o * factor_ref[:, :units]).astype(BF16)
        total_p = total[:, units:] + dot(lowrank_back, da_p[...])
        grad_p = (total_p * factor_ref[:, units:]).astype(BF16)
        lowrank_in = low_in_ref[...]
        sums = contract_last(gb_o[...], grad_o) + contract_last(gb_p[...], grad_p)
        grads_o = contract_first(lowrank_in, grad_o)
        grads_p = contract_first(lowrank_in, grad_p)
        grads_b = contract_first(lowrank_back, hidden_ref[...])
        if last:
            done = sums_before.shape[1]
            sums_ref[:rank, :done] = sums_before[...]
            sums_ref[:rank, done:] = sums
            sums_ref[rank:, :] = sums_back[...]
            grads_ref[:rank, :units] = grads_before[:rank, :units] + grads_o
            grads_ref[:rank, units:] = grads_before[:rank, units:] + grads_p
            grads_ref[rank:, :] = grads_before[rank:, :] + grads_b
        else:
            sums_ref[...] = sums
            grads_ref[:rank, :units] = grads_o
            grads_ref[:rank, units:] = grads_p
            grads_ref[rank:, :] = grads_b


def product_kernel(rank, me_ref, sums_ref, came_ref, *refs):
    sides = ((refs[:5], refs[5:10], refs[10:15]), (refs[15:16], refs[16:21]))
    mine_ref, theirs_ref, buffer, sems = refs[21:]
    span = buffer.shape[2]
    me = me_ref[0]
    plane = lax.div(me, 2)

    def copies(which):
        found, number = [], 0
        begin, end = which * span, (which + 1) * span
        for side, chunks in enumerate(sides):
            base = 0
            for pieces in chunks:
                size = pieces[0].shape[1]
                low, high = max(begin, base), min(end, base + size)
                at = 0
                for piece in pieces:
                    rows = piece.shape[0]
                    if low < high:
                        found.append(
                            pltpu.make_async_copy(
                                piece.at[:, pl.ds(low - base, high - low)],
                                buffer.at[side, pl.ds(at, rows), pl.ds(low - begin, high - low)],
                                sems.at[number],
                            )
                        )
                        number += 1
                    at += rows
                base += size
        return found

    for which in range(4):

        @pl.when(plane == which)
        def _():
            found = copies(which)
            for copy in found:
                copy.start()
            for copy in found:
                copy.wait()

    high, low = halves(sums_ref[...])
    half = span // 2
    even = lax.rem(me, 2) == 0
    crossed = lax.broadcasted_iota(jnp.int32, (rank, span), 1) + plane * span < sides[1][0][0].shape[1]
    for side in range(2):
        at = slice(side * rank, (side + 1) * rank)
        both = jnp.concatenate([high[at], low[at]], axis=0)
        wide = dot(both, buffer[side])
        wide = wide[:rank] + wide[rank:]
        if side == 1:
            moved = dot(dot(both, order_of(came_ref)).astype(BF16), buffer[side])
            wide = jnp.where(crossed, moved[:rank] + moved[rank:], wide)
        mine_ref[side] = jnp.where(even, wide[:, :half], wide[:, half:])
        theirs_ref[side] = jnp.where(even, wide[:, half:], wide[:, :half])


def body(
    tokens,
    cotangent,
    chosen_expert_index,
    router_weight,
    frozen_gate_weight,
    frozen_up_weight,
    frozen_down_weight,
    gate_adapter_first,
    gate_adapter_second,
    down_adapter_first,
    down_adapter_second,
):
    tie = lax.optimization_barrier
    experts = lax.axis_size("dp")
    count, top = chosen_expert_index.shape
    width = tokens.shape[1]
    early = width // DEPTH * EARLY // 7 * DEPTH
    spans, at = [], 0
    for sevenths in CHUNKS:
        size = width // DEPTH * sevenths // 7 * DEPTH
        spans.append((at, size))
        at += size
    capacity = 5 * count * top // (4 * experts)
    slots = experts * capacity
    every = 4 * slots
    gate_w, up_w, down_w = frozen_gate_weight[0], frozen_up_weight[0], frozen_down_weight[0]
    gate_a, gate_b = gate_adapter_first[0], gate_adapter_second[0]
    down_a, down_b = down_adapter_first[0], down_adapter_second[0]
    rank, units = gate_b.shape

    at_row = jnp.arange(every, dtype=jnp.int32)[:, None]
    want = at_row // (4 * capacity) * capacity + at_row % capacity
    quarter = at_row // capacity % 4
    came = at_row % slots // capacity * 4 * capacity + at_row // slots * capacity + at_row % capacity

    code = call(
        functools.partial(code_kernel, experts, capacity), shape((1, count), jnp.int32), 16, moved=1024
    )(chosen_expert_index.reshape(1, count))
    raw, scaled = call(
        scale_kernel,
        (shape((count, early + LANES), BF16), shape((count, width - early), BF16)),
        16,
        moved=4 * count * width,
    )(cotangent, router_weight.reshape(1, count), code)
    raw_steps = first_step(raw)

    def pack(*sources):
        spans = [(first, size) for _, first, size in sources]
        part = sum(size for _, size in spans) // PIECES
        return call(
            functools.partial(pack_kernel, spans),
            shape((every, part), BF16),
            32,
            flops=2 * every * PIECES * count * part,
            moved=2 * (PIECES * count + every) * part,
            grid=(1,),
            in_specs=[whole(1, count), whole(every, 1), whole(every, 1)]
            + [whole(*rows.shape) for rows, _, _ in sources],
            out_specs=whole(every, part),
        )(code, want, quarter, *[rows for rows, _, _ in sources])

    def across_dp(packed):
        sent = packed.reshape(experts, -1, packed.shape[1])
        return lax.all_to_all(sent, "dp", split_axis=0, concat_axis=0, tiled=True).reshape(packed.shape)

    def unpack(got, *sizes):
        return call(
            unpack_kernel,
            tuple(shape((slots, size), BF16) for size in sizes),
            32,
            flops=2 * every * every * got.shape[1],
            moved=4 * every * got.shape[1],
        )(got, came)

    mine = (gate_w, up_w, down_w, jnp.concatenate([gate_b, down_a], axis=0))
    raw_far = second_step(*raw_steps)
    sent = pack(*[(tokens, *span) for span in spans], (scaled, 0, width - early))
    got = across_dp(sent)
    raw_pieces = (raw, *raw_steps, *raw_far)
    wide = early // PIECES
    packed_raw = call(
        pack_raw_kernel,
        shape((every, early), BF16),
        VMEM_MIB,
        flops=2 * every * 4 * count * early,
        moved=2 * (4 * count + every) * early,
        grid=(PIECES,),
        in_specs=[whole(every, 1), whole(every, 1)]
        + [pl.BlockSpec((piece.shape[0], wide), lambda i: (0, i)) for piece in raw_pieces]
        + [
            pl.BlockSpec((piece.shape[0], LANES), lambda i: (0, early // LANES))
            for piece in raw_pieces
        ],
        out_specs=pl.BlockSpec((every, wide), lambda i: (0, i)),
        scratch_shapes=[pltpu.VMEM((every, 4 * count), BF16)],
    )(want, quarter, *raw_pieces, *raw_pieces)
    got, theirs, packed_raw = tie((got, tuple(swap_core(w) for w in mine), packed_raw))
    gate_p, up_p, down_p, small_p = theirs
    small = (gate_b, small_p[:rank], down_a, small_p[rank:])
    *rows, rows_back = unpack(got, *[size for _, size in spans], width - early)

    def piece_specs(pieces):
        return [pl.BlockSpec((piece.shape[0], DEPTH), lambda i: (0, i)) for piece in pieces]

    def tall(first):
        return pl.BlockSpec((DEPTH, units), lambda i: (first // DEPTH + i, 0))

    def flat(rows, first):
        return pl.BlockSpec((rows, DEPTH), lambda i: (0, first // DEPTH + i))

    totals = (shape((every, 2 * units), F32), shape((every, 2 * units), F32), shape((every, rank), F32))
    scratch = [pltpu.VMEM(s.shape, s.dtype) for s in totals]
    def gate_up(chunk, pieces, before):
        begins, last = chunk == 0, chunk == len(spans) - 1
        first, size = spans[chunk]
        outs = totals
        if last:
            outs = (
                shape((every, 2 * units), BF16),
                totals[0],
                shape((every, rank), BF16),
                shape((rank, every), F32),
            )
        extra = (before if before else ()) + (small if last else ())
        return call(
            functools.partial(gate_up_kernel, begins, last),
            outs,
            VMEM_MIB,
            flops=2 * every * size * 4 * units,
            moved=2 * size * (every + 4 * units),
            grid=(size // DEPTH,),
            in_specs=piece_specs(pieces)
            + [tall(first)] * 4
            + [flat(rank, first)]
            + [whole(*value.shape) for value in extra],
            out_specs=tuple(whole(*s.shape) for s in outs),
            scratch_shapes=scratch if last else [],
        )(*pieces, gate_w, gate_p, up_w, up_p, gate_a, *extra)

    packed_raw, rows[0] = tie((packed_raw, rows[0]))
    got_raw = across_dp(packed_raw)
    steps_0 = first_step(rows[0])
    steps_0, rows[1] = tie((steps_0, rows[1]))
    far_0 = second_step(*steps_0)
    steps_1 = first_step(rows[1])
    steps_1, far_0, rows[2] = tie((steps_1, far_0, rows[2]))
    far_1 = second_step(*steps_1)
    steps_2 = first_step(rows[2])
    pieces_0 = (rows[0], *steps_0, *far_0)
    part_0 = gate_up(0, pieces_0, None)
    steps_2, part_0 = tie((steps_2, part_0))
    far_2 = second_step(*steps_2)
    pieces_1 = (rows[1], *steps_1, *far_1)
    part_1 = gate_up(1, pieces_1, part_0)
    far_2, part_1, rows_back = tie((far_2, part_1, rows_back))
    steps_3 = first_step(rows_back)
    pieces_2 = (rows[2], *steps_2, *far_2)
    hidden, factor, low_in, sums_back = gate_up(2, pieces_2, part_1)
    steps_3, hidden = tie((steps_3, hidden))
    far_3 = second_step(*steps_3)

    back_0, low_0 = call(
        raw_kernel,
        (totals[0], totals[2]),
        VMEM_MIB,
        flops=2 * every * early * 2 * units,
        moved=2 * early * (every + 2 * units),
        grid=(early // DEPTH,),
        in_specs=[
            pl.BlockSpec((every, DEPTH), lambda i: (0, i)),
            whole(every, 1),
            flat(units, 0),
            flat(units, 0),
            flat(rank, 0),
        ],
        out_specs=(whole(every, 2 * units), whole(every, rank)),
        scratch_shapes=[scratch[0], scratch[2]],
    )(got_raw, came, down_w, down_p, down_b)

    def back(last, pieces, at, *before):
        rows = sum(piece.shape[0] for piece in pieces)

        def block(columns):
            return pl.BlockSpec((rows, columns), lambda i: (at // rows, 0))

        outs = (shape((2 * rank if last else rank, every if last else rows), F32), shape((2 * rank, 2 * units), F32))
        return call(
            functools.partial(back_kernel, last, len(pieces)),
            outs,
            VMEM_MIB,
            flops=2 * rows * (width - early) * 2 * units,
            moved=2 * (width - early) * (rows + 2 * units),
            grid=((width - early) // DEPTH,),
            in_specs=piece_specs(pieces)
            + [flat(units, early)] * 2
            + [flat(rank, early)]
            + [block(2 * units), block(rank), block(2 * units), block(2 * units), block(rank)]
            + [whole(rank, units)] * 4
            + [whole(*value.shape) for value in before],
            out_specs=tuple(whole(*s.shape) for s in outs),
            scratch_shapes=[pltpu.VMEM((rows, 2 * units), F32), pltpu.VMEM((rows, rank), F32)],
        )(*pieces, down_w, down_p, down_b, back_0, low_0, factor, hidden, low_in, *small, *before)

    pieces_3 = (rows_back, *steps_3, *far_3)
    near = back(False, pieces_3[:3], 0)
    sums, grads = back(True, pieces_3[3:], 3 * slots, *near, sums_back)

    def in_order(value, order):
        return jnp.concatenate([value[:, i * slots : (i + 1) * slots] for i in order], axis=1)

    sums = (
        sums
        + in_order(shift_y(sums, 1), (2, 0, 3, 1))
        + in_order(shift_y(sums, -1), (1, 3, 0, 2))
        + in_order(shift_y(sums, 2), (3, 2, 1, 0))
    )
    me = lax.axis_index("seq").astype(jnp.int32).reshape(1)
    share = width // lax.axis_size("seq")
    anywhere = pl.BlockSpec(memory_space=pl.ANY)
    chunks = (*pieces_0, *pieces_1, *pieces_2, got_raw, *pieces_3)
    own, other = call(
        functools.partial(product_kernel, rank),
        (shape((2, rank, share), F32),) * 2,
        VMEM_MIB,
        flops=8 * rank * every * share,
        moved=8 * every * share,
        in_specs=[pl.BlockSpec(memory_space=pltpu.SMEM), whole(2 * rank, every), whole(every, 1)]
        + [anywhere] * len(chunks),
        scratch_shapes=[
            pltpu.VMEM((2, every, 2 * share), BF16),
            pltpu.SemaphoreType.DMA((21,)),
        ],
    )(me, sums, came, *chunks)
    result = own + swap_core(other)
    grad_hidden = grads[:, :units] + swap_core(grads[:, units:])
    return (result[:1], grad_hidden[None, :rank], grad_hidden[None, rank:], result[1:])


def solution(mesh):
    return jax.shard_map(
        body,
        mesh=mesh,
        in_specs=(
            P(("dp", "seq"), None),
            P(("dp", "seq"), None),
            P(("dp", "seq"), None),
            P(("dp", "seq"), None),
            P("dp", None, "seq"),
            P("dp", None, "seq"),
            P("dp", "seq", None),
            P("dp", None, None),
            P("dp", None, "seq"),
            P("dp", None, "seq"),
            P("dp", None, None),
        ),
        out_specs=(
            P("dp", None, "seq"),
            P("dp", None, "seq"),
            P("dp", None, "seq"),
            P("dp", None, "seq"),
        ),
        check_vma=False,
    )
```

```python
import functools
import math

import jax
import jax.numpy as jnp
from jax import lax
from jax.experimental import pallas as pl
from jax.experimental.pallas import tpu as pltpu
from jax.sharding import PartitionSpec as P

PIECES = 4
FIRST = 4
UNIT = 1024
LANES = 128
COVER = 8
MIB = 1 << 20
VMEM_MIB = 58
BF16, F32 = jnp.bfloat16, jnp.float32


def dot(left, right):
    return jnp.dot(left, right, preferred_element_type=F32)


def contract_last(left, right):
    return lax.dot_general(left, right, (((1,), (1,)), ((), ())), preferred_element_type=F32)


def contract_first(left, right):
    return lax.dot_general(left, right, (((0,), (0,)), ((), ())), preferred_element_type=F32)


def shift_y(value, step):
    size = lax.axis_size("seq")
    planes = size // 2
    pairs = [
        (y * 2 + c, ((y + step) % planes) * 2 + c) for y in range(planes) for c in range(2)
    ]
    return lax.ppermute(value, "seq", pairs)


def swap_core(value):
    size = lax.axis_size("seq")
    return lax.ppermute(value, "seq", [(i, i ^ 1) for i in range(size)])


def first_step(rows):
    return shift_y(rows, 1), shift_y(rows, -1)


def split_kernel(before_ref, after_ref, low_ref, high_ref):
    low_ref[...] = before_ref[...]
    high_ref[...] = after_ref[...]


def second_step(before, after):
    rows, columns = before.shape[0] // 2, before.shape[1]
    part = pl.BlockSpec((rows, columns), lambda i: (0, 0))
    low, high = call(
        split_kernel,
        (shape((rows, columns), before.dtype),) * 2,
        16,
        moved=2 * before.size,
        grid=(1,),
        in_specs=[part, pl.BlockSpec((rows, columns), lambda i: (1, 0))],
        out_specs=(part,) * 2,
    )(before, after)
    return shift_y(low, 1), shift_y(high, -1)


def shape(dims, dtype):
    return jax.ShapeDtypeStruct(dims, dtype)


def call(kernel, outs, mib, flops=0, moved=0, **rest):
    return pl.pallas_call(
        kernel,
        out_shape=outs,
        compiler_params=pltpu.CompilerParams(vmem_limit_bytes=mib * MIB),
        cost_estimate=pl.CostEstimate(flops=COVER * flops, bytes_accessed=COVER * moved, transcendentals=0),
        **rest,
    )


def whole(*dims):
    return pl.BlockSpec(dims, lambda *_: (0,) * len(dims))


def scale_kernel(cot_ref, weight_ref, code_ref, rest_ref, raw_ref):
    count = weight_ref.shape[1]
    column = jnp.broadcast_to(weight_ref[...], (count, count)).T[:, :1]
    rest = rest_ref.shape[1]
    late = cot_ref.shape[1] - rest
    for base, size, out in ((rest, late, raw_ref), (0, rest, rest_ref)):
        for at in range(0, size, 512):
            block = cot_ref[:, base + at : base + at + 512].astype(F32)
            out[:, at : at + 512] = (block * column).astype(BF16)
    codes = jnp.broadcast_to(code_ref[...], (count, count)).astype(F32).T
    raw_ref[:, late:] = codes[:, : raw_ref.shape[1] - late].astype(BF16)


def code_kernel(experts, capacity, ids_ref, code_ref):
    ids = ids_ref[...]
    count = ids.shape[1]
    onehot = (lax.broadcasted_iota(jnp.int32, (experts, count), 0) == ids).astype(F32)
    ahead = (
        lax.broadcasted_iota(jnp.int32, (count, count), 0)
        < lax.broadcasted_iota(jnp.int32, (count, count), 1)
    ).astype(BF16)
    earlier = dot(onehot.astype(BF16), ahead)
    slot = jnp.sum(earlier * onehot, axis=0, keepdims=True).astype(jnp.int32)
    code_ref[...] = ids * capacity + slot


def pack_kernel(spans, code_ref, want_ref, piece_ref, *refs):
    out = refs[-1]
    hit = code_ref[...] == want_ref[...]
    placing = jnp.concatenate(
        [(hit & (piece_ref[...] == q)).astype(BF16) for q in range(PIECES)], axis=1
    )
    at = 0
    for rows, (first, size) in zip(refs, spans):
        part = size // PIECES
        stacked = jnp.concatenate(
            [rows[:, first + q * part : first + (q + 1) * part] for q in range(PIECES)], axis=0
        )
        out[:, at : at + part] = dot(placing, stacked).astype(BF16)
        at += part


def unpack_kernel(got_ref, came_ref, *outs):
    count = got_ref.shape[0]
    take = (
        lax.broadcasted_iota(jnp.int32, (count, count), 1) == came_ref[...]
    ).astype(BF16)
    rows = count // PIECES
    at = 0
    for out in outs:
        part = out.shape[1] // PIECES
        taken = dot(take, got_ref[:, at : at + part]).astype(BF16)
        for q in range(PIECES):
            out[:, q * part : (q + 1) * part] = taken[q * rows : (q + 1) * rows]
        at += part


def pack_raw_kernel(want_ref, plane_ref, *refs):
    pieces, codes, out, placing = refs[:5], refs[5:10], refs[10], refs[11]

    @pl.when(pl.program_id(0) == 0)
    def _():
        code = jnp.concatenate([piece[...] for piece in codes], axis=0).astype(F32)
        count = code.shape[0] // 4
        for k in range(4):
            row = code[k * count : (k + 1) * count].T[:1].astype(jnp.int32)
            hit = (row == want_ref[...]) & (plane_ref[...] == k)
            placing[:, k * count : (k + 1) * count] = hit.astype(BF16)

    stacked = jnp.concatenate([piece[...] for piece in pieces], axis=0)
    out[...] = dot(placing[...], stacked).astype(BF16)


def gate_up_kernel(begins, last, *refs):
    pieces, (gate_o, gate_p, up_o, up_p, first) = refs[:5], refs[5:10]
    refs = refs[10:]
    if not begins:
        prev, refs = refs[:3], refs[3:]
    if last:
        (gb_o, gb_p, da_o, da_p), refs = refs[:4], refs[4:]
        (hidden_ref, factor_ref, low_ref, sums_ref), refs = refs[:4], refs[4:]
    gate, up, low = refs
    step = pl.program_id(0)
    units = gate_o.shape[1]

    @pl.when(step == 0)
    def _():
        for i, total in enumerate((gate, up, low)):
            total[...] = jnp.zeros_like(total) if begins else prev[i][...]

    rows = jnp.concatenate([piece[...] for piece in pieces], axis=0)
    gate[:, :units] += dot(rows, gate_o[...])
    gate[:, units:] += dot(rows, gate_p[...])
    up[:, :units] += dot(rows, up_o[...])
    up[:, units:] += dot(rows, up_p[...])
    low[...] += contract_last(rows, first[...])

    if last:

        @pl.when(step == pl.num_programs(0) - 1)
        def _():
            lowrank_in = low[...].astype(BF16)
            low_ref[...] = lowrank_in
            gate[:, :units] += dot(lowrank_in, gb_o[...])
            gate[:, units:] += dot(lowrank_in, gb_p[...])
            block = 32

            def some(i, carry):
                at = pl.ds(pl.multiple_of(i * block, block), block)
                gate_pre, up_pre = gate[at, :], up[at, :]
                sigmoid_val = jax.nn.sigmoid(gate_pre)
                slope = up_pre * sigmoid_val
                hidden_ref[at, :] = (gate_pre * slope).astype(BF16)
                factor_ref[at, :] = slope * (1.0 + gate_pre * (1.0 - sigmoid_val))
                return carry

            lax.fori_loop(0, gate.shape[0] // block, some, 0)
            sums_ref[...] = contract_last(da_o[...], hidden_ref[:, :units]) + contract_last(
                da_p[...], hidden_ref[:, units:]
            )


def halves(value):
    high = value.astype(BF16)
    return high, (value - high.astype(F32)).astype(BF16)


def order_of(came_ref):
    count = came_ref.shape[0]
    return (lax.broadcasted_iota(jnp.int32, (count, count), 1) == came_ref[...]).astype(BF16)


def raw_kernel(got_ref, came_ref, down_o, down_p, first, total_ref, low_ref, total, low):
    units = down_o.shape[0]
    step = pl.program_id(0)

    @pl.when(step == 0)
    def _():
        total[...] = jnp.zeros_like(total)
        low[...] = jnp.zeros_like(low)

    rows = got_ref[...]
    total[:, :units] += contract_last(rows, down_o[...])
    total[:, units:] += contract_last(rows, down_p[...])
    low[...] += contract_last(rows, first[...])

    @pl.when(step == pl.num_programs(0) - 1)
    def _():
        order = order_of(came_ref)
        for source, out in ((total, total_ref), (low, low_ref)):
            high_part, low_part = halves(source[...])
            out[...] = dot(order, high_part) + dot(order, low_part)


def back_kernel(last, pieces, *refs):
    refs = list(refs)

    def take(number):
        taken = refs[:number]
        del refs[:number]
        return taken

    rows_refs, (down_o, down_p, first) = take(pieces), take(3)
    prev, (factor_ref, hidden_ref, low_in_ref) = take(2), take(3)
    gb_o, gb_p, da_o, da_p = take(4)
    if last:
        sums_before, *grads_before, sums_back = take(4)
    sums_ref, grads_o_ref, grads_p_ref, total, low = refs
    step = pl.program_id(0)
    units = down_o.shape[0]

    @pl.when(step == 0)
    def _():
        total[...] = prev[0][...]
        low[...] = prev[1][...]

    rows = jnp.concatenate([piece[...] for piece in rows_refs], axis=0)
    total[:, :units] += contract_last(rows, down_o[...])
    total[:, units:] += contract_last(rows, down_p[...])
    low[...] += contract_last(rows, first[...])

    @pl.when(step == pl.num_programs(0) - 1)
    def _():
        lowrank_back = low[...].astype(BF16)
        rank = lowrank_back.shape[1]
        total_o = total[:, :units] + dot(lowrank_back, da_o[...])
        grad_o = (total_o * factor_ref[:, :units]).astype(BF16)
        total_p = total[:, units:] + dot(lowrank_back, da_p[...])
        grad_p = (total_p * factor_ref[:, units:]).astype(BF16)
        lowrank_in = low_in_ref[...]
        sums = contract_last(gb_o[...], grad_o) + contract_last(gb_p[...], grad_p)
        grads_o = contract_first(lowrank_in, grad_o)
        grads_p = contract_first(lowrank_in, grad_p)
        grads_b = contract_first(lowrank_back, hidden_ref[...])
        if last:
            done = sums_before.shape[1]
            sums_ref[:rank, :done] = sums_before[...]
            sums_ref[:rank, done:] = sums
            sums_ref[rank:, :] = sums_back[...]
        else:
            sums_ref[...] = sums
        for i, (out, top) in enumerate(((grads_o_ref, grads_o), (grads_p_ref, grads_p))):
            bottom = grads_b[:, i * units : (i + 1) * units]
            if last:
                top = top + grads_before[i][:rank, :]
                bottom = bottom + grads_before[i][rank:, :]
            out[:rank, :] = top
            out[rank:, :] = bottom


def select_kernel(counts, me_ref, *refs):
    number = sum(sum(side) for side in counts)
    ins, outs, sems = list(refs[:number]), refs[number:-1], refs[-1]
    sides = [[[ins.pop(0) for _ in range(pieces)] for pieces in side] for side in counts]
    span = outs[0].shape[1]
    plane = lax.div(me_ref[0], 2)

    def copies(which):
        found = []
        begin, end = which * span, (which + 1) * span
        for chunks, out in zip(sides, outs):
            base = 0
            for pieces in chunks:
                size = pieces[0].shape[1]
                low, high = max(begin, base), min(end, base + size)
                at = 0
                for piece in pieces:
                    rows = piece.shape[0]
                    if low < high:
                        found.append(
                            pltpu.make_async_copy(
                                piece.at[:, pl.ds(low - base, high - low)],
                                out.at[pl.ds(at, rows), pl.ds(low - begin, high - low)],
                                sems.at[len(found)],
                            )
                        )
                    at += rows
                base += size
        return found

    for which in range(4):

        @pl.when(plane == which)
        def _():
            found = copies(which)
            for copy in found:
                copy.start()
            for copy in found:
                copy.wait()


def product_kernel(rest, me_ref, came_ref, tok_ref, cot_ref, own_ref, *refs):
    others, (mine_ref, theirs_ref) = refs[:3], refs[3:]
    rank, span = mine_ref.shape[1], tok_ref.shape[1]
    slots = tok_ref.shape[0] // 4
    me = me_ref[0]
    sums = own_ref[...]
    for other, order in zip(others, ((2, 0, 3, 1), (1, 3, 0, 2), (3, 2, 1, 0))):
        value = other[...]
        sums = sums + jnp.concatenate([value[:, i * slots : (i + 1) * slots] for i in order], axis=1)
    high, low = halves(sums)
    half = span // 2
    even = lax.rem(me, 2) == 0
    crossed = lax.broadcasted_iota(jnp.int32, (rank, span), 1) + lax.div(me, 2) * span >= rest
    for side, rows_ref in enumerate((tok_ref, cot_ref)):
        at = slice(side * rank, (side + 1) * rank)
        both = jnp.concatenate([high[at], low[at]], axis=0)
        rows = rows_ref[...]
        if side == 1:
            both = jnp.concatenate([both, dot(both, order_of(came_ref)).astype(BF16)], axis=0)
        wide = dot(both, rows)
        if side == 1:
            moved = wide[2 * rank : 3 * rank] + wide[3 * rank :]
        wide = wide[:rank] + wide[rank : 2 * rank]
        if side == 1:
            wide = jnp.where(crossed, moved, wide)
        mine_ref[side] = jnp.where(even, wide[:, :half], wide[:, half:])
        theirs_ref[side] = jnp.where(even, wide[:, half:], wide[:, :half])


def final_kernel(own_ref, other_ref, grads_ref, more_ref, ga_ref, gb_ref, da_ref, db_ref):
    rank = ga_ref.shape[1]
    ga_ref[0] = own_ref[0] + other_ref[0]
    db_ref[0] = own_ref[1] + other_ref[1]
    gb_ref[0] = grads_ref[:rank, :] + more_ref[:rank, :]
    da_ref[0] = grads_ref[rank:, :] + more_ref[rank:, :]


def body(
    tokens,
    cotangent,
    chosen_expert_index,
    router_weight,
    frozen_gate_weight,
    frozen_up_weight,
    frozen_down_weight,
    gate_adapter_first,
    gate_adapter_second,
    down_adapter_first,
    down_adapter_second,
):
    tie = lax.optimization_barrier
    experts = lax.axis_size("dp")
    count, top = chosen_expert_index.shape
    width = tokens.shape[1]
    first = width // UNIT * FIRST // 7 * UNIT
    spans = ((0, first), (first, width - first))
    rest, late = first, width - first
    capacity = 5 * count * top // (4 * experts)
    slots = experts * capacity
    every = 4 * slots
    gate_w, up_w, down_w = frozen_gate_weight[0], frozen_up_weight[0], frozen_down_weight[0]
    gate_a, gate_b = gate_adapter_first[0], gate_adapter_second[0]
    down_a, down_b = down_adapter_first[0], down_adapter_second[0]
    rank, units = gate_b.shape

    at_row = jnp.arange(every, dtype=jnp.int32)[:, None]
    want = at_row // (4 * capacity) * capacity + at_row % capacity
    quarter = at_row // capacity % 4
    came = at_row % slots // capacity * 4 * capacity + at_row // slots * capacity + at_row % capacity

    code = call(
        functools.partial(code_kernel, experts, capacity), shape((1, count), jnp.int32), 16, moved=1024
    )(chosen_expert_index.reshape(1, count))
    scaled, raw = call(
        scale_kernel,
        (shape((count, rest), BF16), shape((count, late + LANES), BF16)),
        16,
        moved=4 * count * width,
    )(cotangent, router_weight.reshape(1, count), code)
    raw_steps = first_step(raw)

    def pack(code, *sources):
        spans = [(first, size) for _, first, size in sources]
        part = sum(size for _, size in spans) // PIECES
        return call(
            functools.partial(pack_kernel, spans),
            shape((every, part), BF16),
            VMEM_MIB,
            flops=2 * every * PIECES * count * part,
            moved=2 * (PIECES * count + every) * part,
            grid=(1,),
            in_specs=[whole(1, count), whole(every, 1), whole(every, 1)]
            + [whole(*rows.shape) for rows, _, _ in sources],
            out_specs=whole(every, part),
        )(code, want, quarter, *[rows for rows, _, _ in sources])

    def across_dp(packed):
        sent = packed.reshape(experts, -1, packed.shape[1])
        return lax.all_to_all(sent, "dp", split_axis=0, concat_axis=0, tiled=True).reshape(packed.shape)

    def unpack(got, *sizes):
        return call(
            unpack_kernel,
            tuple(shape((slots, size), BF16) for size in sizes),
            VMEM_MIB,
            flops=2 * every * every * got.shape[1] // COVER,
            moved=4 * every * got.shape[1] // COVER,
        )(got, came)

    mine = (gate_w, up_w, down_w, jnp.concatenate([gate_b, down_a], axis=0))
    got = across_dp(pack(code, (tokens, *spans[0])))
    code, raw_steps = tie((code, raw_steps))
    raw_far = second_step(*raw_steps)
    sent = pack(code, (tokens, *spans[1]), (scaled, 0, rest))
    got, sent = tie((got, sent))
    (rows_0,) = unpack(got, first)
    rows_0, sent = tie((rows_0, sent))
    steps_0 = first_step(rows_0)
    got = across_dp(sent)
    raw_far, steps_0 = tie((raw_far, steps_0))
    far_0 = second_step(*steps_0)

    raw_pieces = (raw, *raw_steps, *raw_far)
    wide = late // PIECES
    packed_raw = call(
        pack_raw_kernel,
        shape((every, late), BF16),
        VMEM_MIB,
        flops=2 * every * 4 * count * late,
        moved=2 * (4 * count + every) * late,
        grid=(PIECES,),
        in_specs=[whole(every, 1), whole(every, 1)]
        + [pl.BlockSpec((piece.shape[0], wide), lambda i: (0, i)) for piece in raw_pieces]
        + [
            pl.BlockSpec((piece.shape[0], LANES), lambda i: (0, late // LANES))
            for piece in raw_pieces
        ],
        out_specs=pl.BlockSpec((every, wide), lambda i: (0, i)),
        scratch_shapes=[pltpu.VMEM((every, 4 * count), BF16)],
    )(want, quarter, *raw_pieces, *raw_pieces)
    got, theirs, packed_raw = tie((got, tuple(swap_core(w) for w in mine), packed_raw))
    gate_p, up_p, down_p, small_p = theirs
    small = (gate_b, small_p[:rank], down_a, small_p[rank:])
    rows_1, rows_2 = unpack(got, width - first, rest)

    def piece_specs(pieces, depth):
        return [pl.BlockSpec((piece.shape[0], depth), lambda i: (0, i)) for piece in pieces]

    def tall(depth, first):
        return pl.BlockSpec((depth, units), lambda i: (first // depth + i, 0))

    def flat(rows, depth, first):
        return pl.BlockSpec((rows, depth), lambda i: (0, first // depth + i))

    totals = (shape((every, 2 * units), F32), shape((every, 2 * units), F32), shape((every, rank), F32))
    scratch = [pltpu.VMEM(s.shape, s.dtype) for s in totals]
    def gate_up(chunk, pieces, before):
        begins, last = chunk == 0, chunk == len(spans) - 1
        first, size = spans[chunk]
        depth = math.gcd(first, size) if first else size // 2
        outs = totals
        if last:
            outs = (
                shape((every, 2 * units), BF16),
                totals[0],
                shape((every, rank), BF16),
                shape((rank, every), F32),
            )
        extra = (before if before else ()) + (small if last else ())
        return call(
            functools.partial(gate_up_kernel, begins, last),
            outs,
            VMEM_MIB,
            flops=2 * every * size * 4 * units,
            moved=2 * size * (every + 4 * units),
            grid=(size // depth,),
            in_specs=piece_specs(pieces, depth)
            + [tall(depth, first)] * 4
            + [flat(rank, depth, first)]
            + [whole(*value.shape) for value in extra],
            out_specs=tuple(whole(*s.shape) for s in outs),
            scratch_shapes=scratch if last else [],
        )(*pieces, gate_w, gate_p, up_w, up_p, gate_a, *extra)

    packed_raw, rows_1, far_0 = tie((packed_raw, rows_1, far_0))
    got_raw = across_dp(packed_raw)
    steps_1 = first_step(rows_1)
    steps_1, rows_0 = tie((steps_1, rows_0))
    pieces_0 = (rows_0, *steps_0, *far_0)
    part_0 = gate_up(0, pieces_0, None)
    far_1 = second_step(*steps_1)
    far_1, rows_2 = tie((far_1, rows_2))
    steps_2 = first_step(rows_2)
    pieces_1 = (rows_1, *steps_1, *far_1)
    hidden, factor, low_in, sums_back = gate_up(1, pieces_1, part_0)
    steps_2, hidden = tie((steps_2, hidden))
    far_2 = second_step(*steps_2)

    depth = math.gcd(rest, late)
    back_0, low_0 = call(
        raw_kernel,
        (totals[0], totals[2]),
        VMEM_MIB,
        flops=2 * every * late * 2 * units,
        moved=2 * late * (every + 2 * units),
        grid=(late // depth,),
        in_specs=[
            pl.BlockSpec((every, depth), lambda i: (0, i)),
            whole(every, 1),
            flat(units, depth, rest),
            flat(units, depth, rest),
            flat(rank, depth, rest),
        ],
        out_specs=(whole(every, 2 * units), whole(every, rank)),
        scratch_shapes=[scratch[0], scratch[2]],
    )(got_raw, came, down_w, down_p, down_b)

    def back(last, pieces, at, *before):
        rows = sum(piece.shape[0] for piece in pieces)

        def block(columns):
            return pl.BlockSpec((rows, columns), lambda i: (at // rows, 0))

        outs = (
            shape((2 * rank if last else rank, every if last else rows), F32),
            *[shape((2 * rank, units), F32)] * 2,
        )
        depth = rest // 2
        return call(
            functools.partial(back_kernel, last, len(pieces)),
            outs,
            VMEM_MIB,
            flops=2 * rows * rest * 2 * units,
            moved=2 * rest * (rows + 2 * units),
            grid=(rest // depth,),
            in_specs=piece_specs(pieces, depth)
            + [flat(units, depth, 0)] * 2
            + [flat(rank, depth, 0)]
            + [block(2 * units), block(rank), block(2 * units), block(2 * units), block(rank)]
            + [whole(rank, units)] * 4
            + [whole(*value.shape) for value in before],
            out_specs=tuple(whole(*s.shape) for s in outs),
            scratch_shapes=[pltpu.VMEM((rows, 2 * units), F32), pltpu.VMEM((rows, rank), F32)],
        )(*pieces, down_w, down_p, down_b, back_0, low_0, factor, hidden, low_in, *small, *before)

    pieces_2 = (rows_2, *steps_2, *far_2)
    near = back(False, pieces_2[:3], 0)
    sums, grads, for_other = back(True, pieces_2[3:], 3 * slots, *near, sums_back)

    me = lax.axis_index("seq").astype(jnp.int32).reshape(1)
    share = width // lax.axis_size("seq")
    scalar = pl.BlockSpec(memory_space=pltpu.SMEM)
    chunks = (*pieces_0, *pieces_1, *pieces_2, got_raw)
    tok, cot = call(
        functools.partial(select_kernel, ((5, 5), (5, 1))),
        (shape((every, 2 * share), BF16),) * 2,
        VMEM_MIB,
        moved=16 * every * share,
        in_specs=[scalar] + [pl.BlockSpec(memory_space=pl.ANY)] * len(chunks),
        out_specs=(whole(every, 2 * share),) * 2,
        scratch_shapes=[pltpu.SemaphoreType.DMA((len(chunks),))],
    )(me, *chunks)
    own, other = call(
        functools.partial(product_kernel, rest),
        (shape((2, rank, share), F32),) * 2,
        16,
        flops=8 * rank * every * share,
        moved=8 * every * share,
        in_specs=[scalar, whole(every, 1)]
        + [whole(every, 2 * share)] * 2
        + [whole(2 * rank, every)] * 4,
    )(me, came, tok, cot, sums, shift_y(sums, 1), shift_y(sums, -1), shift_y(sums, 2))
    return tuple(
        call(
            final_kernel,
            (
                shape((1, rank, share), F32),
                shape((1, rank, units), F32),
                shape((1, rank, units), F32),
                shape((1, rank, share), F32),
            ),
            8,
            moved=24 * rank * share,
        )(own, swap_core(other), grads, swap_core(for_other))
    )


def solution(mesh):
    return jax.shard_map(
        body,
        mesh=mesh,
        in_specs=(
            P(("dp", "seq"), None),
            P(("dp", "seq"), None),
            P(("dp", "seq"), None),
            P(("dp", "seq"), None),
            P("dp", None, "seq"),
            P("dp", None, "seq"),
            P("dp", "seq", None),
            P("dp", None, None),
            P("dp", None, "seq"),
            P("dp", None, "seq"),
            P("dp", None, None),
        ),
        out_specs=(
            P("dp", None, "seq"),
            P("dp", None, "seq"),
            P("dp", None, "seq"),
            P("dp", None, "seq"),
        ),
        check_vma=False,
    )
```

```python
import functools
import math

import jax
import jax.numpy as jnp
import numpy as np
from jax import lax
from jax.experimental import pallas as pl
from jax.experimental.pallas import tpu as pltpu
from jax.sharding import PartitionSpec as P

PIECES = 4
FIRST = 4
UNIT = 1024
LANES = 128
COVER = 8
MIB = 1 << 20
VMEM_MIB = 58
BF16, F32 = jnp.bfloat16, jnp.float32


def dot(left, right):
    return jnp.dot(left, right, preferred_element_type=F32)


def contract_last(left, right):
    return lax.dot_general(left, right, (((1,), (1,)), ((), ())), preferred_element_type=F32)


def contract_first(left, right):
    return lax.dot_general(left, right, (((0,), (0,)), ((), ())), preferred_element_type=F32)


def shift_y(value, step):
    size = lax.axis_size("seq")
    planes = size // 2
    pairs = [
        (y * 2 + c, ((y + step) % planes) * 2 + c) for y in range(planes) for c in range(2)
    ]
    return lax.ppermute(value, "seq", pairs)


def swap_core(value):
    size = lax.axis_size("seq")
    return lax.ppermute(value, "seq", [(i, i ^ 1) for i in range(size)])


def first_step(rows):
    return shift_y(rows, 1), shift_y(rows, -1)


def split_kernel(before_ref, after_ref, low_ref, high_ref):
    low_ref[...] = before_ref[...]
    high_ref[...] = after_ref[...]


def second_step(before, after):
    rows, columns = before.shape[0] // 2, before.shape[1]
    part = pl.BlockSpec((rows, columns), lambda i: (0, 0))
    low, high = call(
        split_kernel,
        (shape((rows, columns), before.dtype),) * 2,
        16,
        moved=2 * before.size,
        grid=(1,),
        in_specs=[part, pl.BlockSpec((rows, columns), lambda i: (1, 0))],
        out_specs=(part,) * 2,
    )(before, after)
    return shift_y(low, 1), shift_y(high, -1)


def shape(dims, dtype):
    return jax.ShapeDtypeStruct(dims, dtype)


def call(kernel, outs, mib, flops=0, moved=0, **rest):
    return pl.pallas_call(
        kernel,
        out_shape=outs,
        compiler_params=pltpu.CompilerParams(vmem_limit_bytes=mib * MIB),
        cost_estimate=pl.CostEstimate(flops=COVER * flops, bytes_accessed=COVER * moved, transcendentals=0),
        **rest,
    )


def whole(*dims):
    return pl.BlockSpec(dims, lambda *_: (0,) * len(dims))


def scale_kernel(cot_ref, weight_ref, code_ref, rest_ref, raw_ref):
    count = weight_ref.shape[1]
    column = jnp.broadcast_to(weight_ref[...], (count, count)).T[:, :1]
    rest = rest_ref.shape[1]
    late = cot_ref.shape[1] - rest
    for base, size, out in ((rest, late, raw_ref), (0, rest, rest_ref)):
        for at in range(0, size, 512):
            block = cot_ref[:, base + at : base + at + 512].astype(F32)
            out[:, at : at + 512] = (block * column).astype(BF16)
    codes = jnp.broadcast_to(code_ref[...], (count, count)).astype(F32).T
    raw_ref[:, late:] = codes[:, : raw_ref.shape[1] - late].astype(BF16)


def code_kernel(experts, capacity, ids_ref, code_ref):
    ids = ids_ref[...]
    count = ids.shape[1]
    onehot = (lax.broadcasted_iota(jnp.int32, (experts, count), 0) == ids).astype(F32)
    ahead = (
        lax.broadcasted_iota(jnp.int32, (count, count), 0)
        < lax.broadcasted_iota(jnp.int32, (count, count), 1)
    ).astype(BF16)
    earlier = dot(onehot.astype(BF16), ahead)
    slot = jnp.sum(earlier * onehot, axis=0, keepdims=True).astype(jnp.int32)
    code_ref[...] = ids * capacity + slot


def pack_kernel(spans, code_ref, want_ref, piece_ref, *refs):
    out = refs[-1]
    hit = code_ref[...] == want_ref[...]
    placing = jnp.concatenate(
        [(hit & (piece_ref[...] == q)).astype(BF16) for q in range(PIECES)], axis=1
    )
    at = 0
    for rows, (first, size) in zip(refs, spans):
        part = size // PIECES
        stacked = jnp.concatenate(
            [rows[:, first + q * part : first + (q + 1) * part] for q in range(PIECES)], axis=0
        )
        out[:, at : at + part] = dot(placing, stacked).astype(BF16)
        at += part


def unpack_kernel(got_ref, came_ref, *outs):
    count = got_ref.shape[0]
    take = (
        lax.broadcasted_iota(jnp.int32, (count, count), 1) == came_ref[...]
    ).astype(BF16)
    rows = count // PIECES
    at = 0
    for out in outs:
        part = out.shape[1] // PIECES
        taken = dot(take, got_ref[:, at : at + part]).astype(BF16)
        for q in range(PIECES):
            out[:, q * part : (q + 1) * part] = taken[q * rows : (q + 1) * rows]
        at += part


def pack_raw_kernel(want_ref, plane_ref, *refs):
    pieces, codes, out, placing = refs[:5], refs[5:10], refs[10], refs[11]

    @pl.when(pl.program_id(0) == 0)
    def _():
        code = jnp.concatenate([piece[...] for piece in codes], axis=0).astype(F32)
        count = code.shape[0] // 4
        for k in range(4):
            row = code[k * count : (k + 1) * count].T[:1].astype(jnp.int32)
            hit = (row == want_ref[...]) & (plane_ref[...] == k)
            placing[:, k * count : (k + 1) * count] = hit.astype(BF16)

    stacked = jnp.concatenate([piece[...] for piece in pieces], axis=0)
    out[...] = dot(placing[...], stacked).astype(BF16)


def gate_up_kernel(begins, last, *refs):
    pieces, (gate_o, gate_p, up_o, up_p, first) = refs[:5], refs[5:10]
    refs = refs[10:]
    if not begins:
        prev, refs = refs[:3], refs[3:]
    if last:
        (gb_o, gb_p, da_o, da_p), refs = refs[:4], refs[4:]
        (hidden_ref, factor_ref, low_ref, sums_ref), refs = refs[:4], refs[4:]
    gate, up, low = refs
    step = pl.program_id(0)
    units = gate_o.shape[1]

    @pl.when(step == 0)
    def _():
        for i, total in enumerate((gate, up, low)):
            total[...] = jnp.zeros_like(total) if begins else prev[i][...]

    rows = jnp.concatenate([piece[...] for piece in pieces], axis=0)
    gate[:, :units] += dot(rows, gate_o[...])
    gate[:, units:] += dot(rows, gate_p[...])
    up[:, :units] += dot(rows, up_o[...])
    up[:, units:] += dot(rows, up_p[...])
    low[...] += contract_last(rows, first[...])

    if last:

        @pl.when(step == pl.num_programs(0) - 1)
        def _():
            lowrank_in = low[...].astype(BF16)
            low_ref[...] = lowrank_in
            gate[:, :units] += dot(lowrank_in, gb_o[...])
            gate[:, units:] += dot(lowrank_in, gb_p[...])
            block = 32

            def some(i, carry):
                at = pl.ds(pl.multiple_of(i * block, block), block)
                gate_pre, up_pre = gate[at, :], up[at, :]
                sigmoid_val = jax.nn.sigmoid(gate_pre)
                slope = up_pre * sigmoid_val
                hidden_ref[at, :] = (gate_pre * slope).astype(BF16)
                factor_ref[at, :] = slope * (1.0 + gate_pre * (1.0 - sigmoid_val))
                return carry

            lax.fori_loop(0, gate.shape[0] // block, some, 0)
            sums_ref[...] = contract_last(da_o[...], hidden_ref[:, :units]) + contract_last(
                da_p[...], hidden_ref[:, units:]
            )


def halves(value):
    high = value.astype(BF16)
    return high, (value - high.astype(F32)).astype(BF16)


def order_of(came_ref):
    count = came_ref.shape[0]
    return (lax.broadcasted_iota(jnp.int32, (count, count), 1) == came_ref[...]).astype(BF16)


def raw_kernel(got_ref, came_ref, down_o, down_p, first, total_ref, low_ref, total, low):
    units = down_o.shape[0]
    step = pl.program_id(0)

    @pl.when(step == 0)
    def _():
        total[...] = jnp.zeros_like(total)
        low[...] = jnp.zeros_like(low)

    rows = got_ref[...]
    total[:, :units] += contract_last(rows, down_o[...])
    total[:, units:] += contract_last(rows, down_p[...])
    low[...] += contract_last(rows, first[...])

    @pl.when(step == pl.num_programs(0) - 1)
    def _():
        order = order_of(came_ref)
        for source, out in ((total, total_ref), (low, low_ref)):
            high_part, low_part = halves(source[...])
            out[...] = dot(order, high_part) + dot(order, low_part)


def back_kernel(last, pieces, *refs):
    refs = list(refs)

    def take(number):
        taken = refs[:number]
        del refs[:number]
        return taken

    rows_refs, (down_o, down_p, first) = take(pieces), take(3)
    prev, (factor_ref, hidden_ref, low_in_ref) = take(2), take(3)
    gb_o, gb_p, da_o, da_p = take(4)
    if last:
        sums_before, *grads_before, sums_back = take(4)
    sums_ref, grads_o_ref, grads_p_ref, total, low = refs
    step = pl.program_id(0)
    units = down_o.shape[0]

    @pl.when(step == 0)
    def _():
        total[...] = prev[0][...]
        low[...] = prev[1][...]

    rows = jnp.concatenate([piece[...] for piece in rows_refs], axis=0)
    total[:, :units] += contract_last(rows, down_o[...])
    total[:, units:] += contract_last(rows, down_p[...])
    low[...] += contract_last(rows, first[...])

    @pl.when(step == pl.num_programs(0) - 1)
    def _():
        lowrank_back = low[...].astype(BF16)
        rank = lowrank_back.shape[1]
        total_o = total[:, :units] + dot(lowrank_back, da_o[...])
        grad_o = (total_o * factor_ref[:, :units]).astype(BF16)
        total_p = total[:, units:] + dot(lowrank_back, da_p[...])
        grad_p = (total_p * factor_ref[:, units:]).astype(BF16)
        lowrank_in = low_in_ref[...]
        sums = contract_last(gb_o[...], grad_o) + contract_last(gb_p[...], grad_p)
        grads_o = contract_first(lowrank_in, grad_o)
        grads_p = contract_first(lowrank_in, grad_p)
        grads_b = contract_first(lowrank_back, hidden_ref[...])
        if last:
            done = sums_before.shape[1]
            sums_ref[:rank, :done] = sums_before[...]
            sums_ref[:rank, done:] = sums
            sums_ref[rank:, :] = sums_back[...]
        else:
            sums_ref[...] = sums
        for i, (out, top) in enumerate(((grads_o_ref, grads_o), (grads_p_ref, grads_p))):
            bottom = grads_b[:, i * units : (i + 1) * units]
            if last:
                top = top + grads_before[i][:rank, :]
                bottom = bottom + grads_before[i][rank:, :]
            out[:rank, :] = top
            out[rank:, :] = bottom


def select_kernel(counts, me_ref, *refs):
    number = sum(sum(side) for side in counts)
    ins, outs, sems = list(refs[:number]), refs[number:-1], refs[-1]
    sides = [[[ins.pop(0) for _ in range(pieces)] for pieces in side] for side in counts]
    span = outs[0].shape[1]
    plane = lax.div(me_ref[0], 2)

    def copies(which):
        found = []
        begin, end = which * span, (which + 1) * span
        for chunks, out in zip(sides, outs):
            base = 0
            for pieces in chunks:
                size = pieces[0].shape[1]
                low, high = max(begin, base), min(end, base + size)
                at = 0
                for piece in pieces:
                    rows = piece.shape[0]
                    if low < high:
                        found.append(
                            pltpu.make_async_copy(
                                piece.at[:, pl.ds(low - base, high - low)],
                                out.at[pl.ds(at, rows), pl.ds(low - begin, high - low)],
                                sems.at[len(found)],
                            )
                        )
                    at += rows
                base += size
        return found

    for which in range(4):

        @pl.when(plane == which)
        def _():
            found = copies(which)
            for copy in found:
                copy.start()
            for copy in found:
                copy.wait()


def product_kernel(rest, me_ref, came_ref, tok_ref, cot_ref, own_ref, *refs):
    others, (mine_ref, theirs_ref) = refs[:3], refs[3:]
    rank, span = mine_ref.shape[1], tok_ref.shape[1]
    slots = tok_ref.shape[0] // 4
    me = me_ref[0]
    sums = own_ref[...]
    for other, order in zip(others, ((2, 0, 3, 1), (1, 3, 0, 2), (3, 2, 1, 0))):
        value = other[...]
        sums = sums + jnp.concatenate([value[:, i * slots : (i + 1) * slots] for i in order], axis=1)
    high, low = halves(sums)
    half = span // 2
    even = lax.rem(me, 2) == 0
    crossed = lax.broadcasted_iota(jnp.int32, (rank, span), 1) + lax.div(me, 2) * span >= rest
    for side, rows_ref in enumerate((tok_ref, cot_ref)):
        at = slice(side * rank, (side + 1) * rank)
        both = jnp.concatenate([high[at], low[at]], axis=0)
        rows = rows_ref[...]
        if side == 1:
            both = jnp.concatenate([both, dot(both, order_of(came_ref)).astype(BF16)], axis=0)
        wide = dot(both, rows)
        if side == 1:
            moved = wide[2 * rank : 3 * rank] + wide[3 * rank :]
        wide = wide[:rank] + wide[rank : 2 * rank]
        if side == 1:
            wide = jnp.where(crossed, moved, wide)
        mine_ref[side] = jnp.where(even, wide[:, :half], wide[:, half:])
        theirs_ref[side] = jnp.where(even, wide[:, half:], wide[:, :half])


def final_kernel(own_ref, other_ref, grads_ref, more_ref, ga_ref, gb_ref, da_ref, db_ref):
    rank = ga_ref.shape[1]
    ga_ref[0] = own_ref[0] + other_ref[0]
    db_ref[0] = own_ref[1] + other_ref[1]
    gb_ref[0] = grads_ref[:rank, :] + more_ref[:rank, :]
    da_ref[0] = grads_ref[rank:, :] + more_ref[rank:, :]


def body(
    tokens,
    cotangent,
    chosen_expert_index,
    router_weight,
    frozen_gate_weight,
    frozen_up_weight,
    frozen_down_weight,
    gate_adapter_first,
    gate_adapter_second,
    down_adapter_first,
    down_adapter_second,
):
    tie = lax.optimization_barrier
    experts = lax.axis_size("dp")
    count, top = chosen_expert_index.shape
    width = tokens.shape[1]
    first = width // UNIT * FIRST // 7 * UNIT
    spans = ((0, first), (first, width - first))
    rest, late = first, width - first
    capacity = 5 * count * top // (4 * experts)
    slots = experts * capacity
    every = 4 * slots
    gate_w, up_w, down_w = frozen_gate_weight[0], frozen_up_weight[0], frozen_down_weight[0]
    gate_a, gate_b = gate_adapter_first[0], gate_adapter_second[0]
    down_a, down_b = down_adapter_first[0], down_adapter_second[0]
    rank, units = gate_b.shape

    at_row = np.arange(every, dtype=np.int32)[:, None]
    want = at_row // (4 * capacity) * capacity + at_row % capacity
    quarter = at_row // capacity % 4
    came = at_row % slots // capacity * 4 * capacity + at_row // slots * capacity + at_row % capacity

    code = call(
        functools.partial(code_kernel, experts, capacity), shape((1, count), jnp.int32), 16, moved=1024
    )(chosen_expert_index.reshape(1, count))
    scaled, raw = call(
        scale_kernel,
        (shape((count, rest), BF16), shape((count, late + LANES), BF16)),
        16,
        moved=4 * count * width,
    )(cotangent, router_weight.reshape(1, count), code)
    raw_steps = first_step(raw)

    def pack(code, *sources):
        spans = [(first, size) for _, first, size in sources]
        part = sum(size for _, size in spans) // PIECES
        return call(
            functools.partial(pack_kernel, spans),
            shape((every, part), BF16),
            32,
            flops=2 * every * PIECES * count * part,
            moved=2 * (PIECES * count + every) * part,
            grid=(1,),
            in_specs=[whole(1, count), whole(every, 1), whole(every, 1)]
            + [whole(*rows.shape) for rows, _, _ in sources],
            out_specs=whole(every, part),
        )(code, want, quarter, *[rows for rows, _, _ in sources])

    def across_dp(packed):
        sent = packed.reshape(experts, -1, packed.shape[1])
        return lax.all_to_all(sent, "dp", split_axis=0, concat_axis=0, tiled=True).reshape(packed.shape)

    def unpack(got, *sizes):
        return call(
            unpack_kernel,
            tuple(shape((slots, size), BF16) for size in sizes),
            VMEM_MIB,
            flops=2 * every * every * got.shape[1] // COVER,
            moved=4 * every * got.shape[1] // COVER,
        )(got, came)

    mine = (gate_w, up_w, down_w, jnp.concatenate([gate_b, down_a], axis=0))
    got = across_dp(pack(code, (tokens, *spans[0])))
    code, raw_steps = tie((code, raw_steps))
    raw_far = second_step(*raw_steps)
    sent = pack(code, (tokens, *spans[1]), (scaled, 0, rest))
    got, sent = tie((got, sent))
    (rows_0,) = unpack(got, first)
    rows_0, sent = tie((rows_0, sent))
    steps_0 = first_step(rows_0)
    got = across_dp(sent)
    raw_far, steps_0 = tie((raw_far, steps_0))
    far_0 = second_step(*steps_0)

    raw_pieces = (raw, *raw_steps, *raw_far)
    wide = late // PIECES
    packed_raw = call(
        pack_raw_kernel,
        shape((every, late), BF16),
        VMEM_MIB,
        flops=2 * every * 4 * count * late,
        moved=2 * (4 * count + every) * late,
        grid=(PIECES,),
        in_specs=[whole(every, 1), whole(every, 1)]
        + [pl.BlockSpec((piece.shape[0], wide), lambda i: (0, i)) for piece in raw_pieces]
        + [
            pl.BlockSpec((piece.shape[0], LANES), lambda i: (0, late // LANES))
            for piece in raw_pieces
        ],
        out_specs=pl.BlockSpec((every, wide), lambda i: (0, i)),
        scratch_shapes=[pltpu.VMEM((every, 4 * count), BF16)],
    )(want, quarter, *raw_pieces, *raw_pieces)
    got, theirs, packed_raw = tie((got, tuple(swap_core(w) for w in mine), packed_raw))
    gate_p, up_p, down_p, small_p = theirs
    small = (gate_b, small_p[:rank], down_a, small_p[rank:])
    rows_1, rows_2 = unpack(got, width - first, rest)

    def piece_specs(pieces, depth):
        return [pl.BlockSpec((piece.shape[0], depth), lambda i: (0, i)) for piece in pieces]

    def tall(depth, first):
        return pl.BlockSpec((depth, units), lambda i: (first // depth + i, 0))

    def flat(rows, depth, first):
        return pl.BlockSpec((rows, depth), lambda i: (0, first // depth + i))

    totals = (shape((every, 2 * units), F32), shape((every, 2 * units), F32), shape((every, rank), F32))
    scratch = [pltpu.VMEM(s.shape, s.dtype) for s in totals]
    def gate_up(chunk, pieces, before):
        begins, last = chunk == 0, chunk == len(spans) - 1
        first, size = spans[chunk]
        depth = math.gcd(first, size) if first else size // 2
        outs = totals
        if last:
            outs = (
                shape((every, 2 * units), BF16),
                totals[0],
                shape((every, rank), BF16),
                shape((rank, every), F32),
            )
        extra = (before if before else ()) + (small if last else ())
        return call(
            functools.partial(gate_up_kernel, begins, last),
            outs,
            VMEM_MIB,
            flops=2 * every * size * 4 * units,
            moved=2 * size * (every + 4 * units),
            grid=(size // depth,),
            in_specs=piece_specs(pieces, depth)
            + [tall(depth, first)] * 4
            + [flat(rank, depth, first)]
            + [whole(*value.shape) for value in extra],
            out_specs=tuple(whole(*s.shape) for s in outs),
            scratch_shapes=scratch if last else [],
        )(*pieces, gate_w, gate_p, up_w, up_p, gate_a, *extra)

    rows_1, far_0 = tie((rows_1, far_0))
    got_raw = across_dp(packed_raw)
    steps_1 = first_step(rows_1)
    steps_1, rows_0 = tie((steps_1, rows_0))
    pieces_0 = (rows_0, *steps_0, *far_0)
    part_0 = gate_up(0, pieces_0, None)
    far_1 = second_step(*steps_1)
    far_1, rows_2 = tie((far_1, rows_2))
    steps_2 = first_step(rows_2)
    pieces_1 = (rows_1, *steps_1, *far_1)
    hidden, factor, low_in, sums_back = gate_up(1, pieces_1, part_0)
    depth = math.gcd(rest, late)
    back_0, low_0 = call(
        raw_kernel,
        (totals[0], totals[2]),
        VMEM_MIB,
        flops=2 * every * late * 2 * units,
        moved=2 * late * (every + 2 * units),
        grid=(late // depth,),
        in_specs=[
            pl.BlockSpec((every, depth), lambda i: (0, i)),
            whole(every, 1),
            flat(units, depth, rest),
            flat(units, depth, rest),
            flat(rank, depth, rest),
        ],
        out_specs=(whole(every, 2 * units), whole(every, rank)),
        scratch_shapes=[scratch[0], scratch[2]],
    )(got_raw, came, down_w, down_p, down_b)
    steps_2, hidden, back_0 = tie((steps_2, hidden, back_0))
    far_2 = second_step(*steps_2)

    def back(last, pieces, at, *before):
        rows = sum(piece.shape[0] for piece in pieces)

        def block(columns):
            return pl.BlockSpec((rows, columns), lambda i: (at // rows, 0))

        outs = (
            shape((2 * rank if last else rank, every if last else rows), F32),
            *[shape((2 * rank, units), F32)] * 2,
        )
        depth = rest // 2
        return call(
            functools.partial(back_kernel, last, len(pieces)),
            outs,
            VMEM_MIB,
            flops=2 * rows * rest * 2 * units,
            moved=2 * rest * (rows + 2 * units),
            grid=(rest // depth,),
            in_specs=piece_specs(pieces, depth)
            + [flat(units, depth, 0)] * 2
            + [flat(rank, depth, 0)]
            + [block(2 * units), block(rank), block(2 * units), block(2 * units), block(rank)]
            + [whole(rank, units)] * 4
            + [whole(*value.shape) for value in before],
            out_specs=tuple(whole(*s.shape) for s in outs),
            scratch_shapes=[pltpu.VMEM((rows, 2 * units), F32), pltpu.VMEM((rows, rank), F32)],
        )(*pieces, down_w, down_p, down_b, back_0, low_0, factor, hidden, low_in, *small, *before)

    pieces_2 = (rows_2, *steps_2, *far_2)
    near = back(False, pieces_2[:3], 0)
    sums, grads, for_other = back(True, pieces_2[3:], 3 * slots, *near, sums_back)

    me = lax.axis_index("seq").astype(jnp.int32).reshape(1)
    share = width // lax.axis_size("seq")
    scalar = pl.BlockSpec(memory_space=pltpu.SMEM)
    chunks = (*pieces_0, *pieces_1, *pieces_2, got_raw)
    tok, cot = call(
        functools.partial(select_kernel, ((5, 5), (5, 1))),
        (pltpu.VMEM((every, 2 * share), BF16),) * 2,
        VMEM_MIB,
        moved=16 * every * share,
        in_specs=[scalar] + [pl.BlockSpec(memory_space=pl.ANY)] * len(chunks),
        out_specs=(pl.BlockSpec(memory_space=pltpu.VMEM),) * 2,
        scratch_shapes=[pltpu.SemaphoreType.DMA((len(chunks),))],
    )(me, *chunks)
    own, other = call(
        functools.partial(product_kernel, rest),
        (shape((2, rank, share), F32),) * 2,
        16,
        flops=8 * rank * every * share,
        moved=8 * every * share,
        in_specs=[scalar, whole(every, 1)]
        + [pl.BlockSpec(memory_space=pltpu.VMEM)] * 2
        + [whole(2 * rank, every)] * 4,
    )(me, came, tok, cot, sums, shift_y(sums, 1), shift_y(sums, -1), shift_y(sums, 2))
    return tuple(
        call(
            final_kernel,
            (
                shape((1, rank, share), F32),
                shape((1, rank, units), F32),
                shape((1, rank, units), F32),
                shape((1, rank, share), F32),
            ),
            8,
            moved=24 * rank * share,
        )(own, swap_core(other), grads, swap_core(for_other))
    )


def solution(mesh):
    return jax.shard_map(
        body,
        mesh=mesh,
        in_specs=(
            P(("dp", "seq"), None),
            P(("dp", "seq"), None),
            P(("dp", "seq"), None),
            P(("dp", "seq"), None),
            P("dp", None, "seq"),
            P("dp", None, "seq"),
            P("dp", "seq", None),
            P("dp", None, None),
            P("dp", None, "seq"),
            P("dp", None, "seq"),
            P("dp", None, None),
        ),
        out_specs=(
            P("dp", None, "seq"),
            P("dp", None, "seq"),
            P("dp", None, "seq"),
            P("dp", None, "seq"),
        ),
        check_vma=False,
    )
```

```python
import functools
import math

import jax
import jax.numpy as jnp
from jax import lax
from jax.experimental import pallas as pl
from jax.experimental.pallas import tpu as pltpu
from jax.sharding import PartitionSpec as P

PIECES = 4
FIRST = 4
UNIT = 1024
LANES = 128
COVER = 8
MIB = 1 << 20
VMEM_MIB = 58
BF16, F32 = jnp.bfloat16, jnp.float32


def dot(left, right):
    return jnp.dot(left, right, preferred_element_type=F32)


def contract_last(left, right):
    return lax.dot_general(left, right, (((1,), (1,)), ((), ())), preferred_element_type=F32)


def contract_first(left, right):
    return lax.dot_general(left, right, (((0,), (0,)), ((), ())), preferred_element_type=F32)


def shift_y(value, step):
    size = lax.axis_size("seq")
    planes = size // 2
    pairs = [
        (y * 2 + c, ((y + step) % planes) * 2 + c) for y in range(planes) for c in range(2)
    ]
    return lax.ppermute(value, "seq", pairs)


def swap_core(value):
    size = lax.axis_size("seq")
    return lax.ppermute(value, "seq", [(i, i ^ 1) for i in range(size)])


def first_step(rows):
    return shift_y(rows, 1), shift_y(rows, -1)


def exchanged(value):
    far = shift_y(value, 2)
    return value, shift_y(value, 1), shift_y(value, -1), far


def split_kernel(before_ref, after_ref, low_ref, high_ref):
    low_ref[...] = before_ref[...]
    high_ref[...] = after_ref[...]


def split_rows(before, after):
    rows, columns = before.shape[0] // 2, before.shape[1]
    part = pl.BlockSpec((rows, columns), lambda i: (0, 0))
    return call(
        split_kernel,
        (shape((rows, columns), before.dtype),) * 2,
        16,
        moved=2 * before.size,
        grid=(1,),
        in_specs=[part, pl.BlockSpec((rows, columns), lambda i: (1, 0))],
        out_specs=(part,) * 2,
    )(before, after)


def forward(low, high):
    return shift_y(low, 1), shift_y(high, -1)


def second_step(before, after):
    return forward(*split_rows(before, after))


def shape(dims, dtype):
    return jax.ShapeDtypeStruct(dims, dtype)


def call(kernel, outs, mib, flops=0, moved=0, **rest):
    return pl.pallas_call(
        kernel,
        out_shape=outs,
        compiler_params=pltpu.CompilerParams(vmem_limit_bytes=mib * MIB),
        cost_estimate=pl.CostEstimate(flops=COVER * flops, bytes_accessed=COVER * moved, transcendentals=0),
        **rest,
    )


def whole(*dims):
    return pl.BlockSpec(dims, lambda *_: (0,) * len(dims))


def scale_kernel(cot_ref, weight_ref, code_ref, rest_ref, raw_ref):
    count = weight_ref.shape[1]
    column = jnp.broadcast_to(weight_ref[...], (count, count)).T[:, :1]
    rest = rest_ref.shape[1]
    late = cot_ref.shape[1] - rest
    for base, size, out in ((rest, late, raw_ref), (0, rest, rest_ref)):
        for at in range(0, size, 512):
            block = cot_ref[:, base + at : base + at + 512].astype(F32)
            out[:, at : at + 512] = (block * column).astype(BF16)
    codes = jnp.broadcast_to(code_ref[...], (count, count)).astype(F32).T
    raw_ref[:, late:] = codes[:, : raw_ref.shape[1] - late].astype(BF16)


def index_parts(count, outer, inner):
    row = lax.broadcasted_iota(jnp.int32, (count, 1), 0).astype(F32)
    first = jnp.floor((row + 0.5) * (1.0 / (outer * inner)))
    row = row - first * (outer * inner)
    second = jnp.floor((row + 0.5) * (1.0 / inner))
    return [part.astype(jnp.int32) for part in (first, second, row - second * inner)]


def wanted(count, capacity):
    expert, piece, slot = index_parts(count, 4, capacity)
    return expert * capacity + slot, piece


def order_of(count, capacity):
    piece, source, slot = index_parts(count, count // (4 * capacity), capacity)
    came = source * (4 * capacity) + piece * capacity + slot
    return (lax.broadcasted_iota(jnp.int32, (count, count), 1) == came).astype(BF16)


def code_kernel(experts, capacity, ids_ref, code_ref):
    ids = ids_ref[...]
    count = ids.shape[1]
    onehot = (lax.broadcasted_iota(jnp.int32, (experts, count), 0) == ids).astype(F32)
    ahead = (
        lax.broadcasted_iota(jnp.int32, (count, count), 0)
        < lax.broadcasted_iota(jnp.int32, (count, count), 1)
    ).astype(BF16)
    earlier = dot(onehot.astype(BF16), ahead)
    slot = jnp.sum(earlier * onehot, axis=0, keepdims=True).astype(jnp.int32)
    code_ref[...] = ids * capacity + slot


def pack_kernel(spans, capacity, code_ref, *refs):
    out = refs[-1]
    want, piece = wanted(out.shape[0], capacity)
    hit = code_ref[...] == want
    placing = jnp.concatenate(
        [(hit & (piece == q)).astype(BF16) for q in range(PIECES)], axis=1
    )
    at = 0
    for rows, (first, size) in zip(refs, spans):
        part = size // PIECES
        stacked = jnp.concatenate(
            [rows[:, first + q * part : first + (q + 1) * part] for q in range(PIECES)], axis=0
        )
        out[:, at : at + part] = dot(placing, stacked).astype(BF16)
        at += part


def unpack_kernel(capacity, got_ref, *outs):
    count = got_ref.shape[0]
    take = order_of(count, capacity)
    rows = count // PIECES
    at = 0
    for out in outs:
        part = out.shape[1] // PIECES
        taken = dot(take, got_ref[:, at : at + part]).astype(BF16)
        for q in range(PIECES):
            out[:, q * part : (q + 1) * part] = taken[q * rows : (q + 1) * rows]
        at += part


def pack_raw_kernel(capacity, *refs):
    pieces, codes, out, placing = refs[:5], refs[5:10], refs[10], refs[11]

    @pl.when(pl.program_id(0) == 0)
    def _():
        code = jnp.concatenate([piece[...] for piece in codes], axis=0).astype(F32)
        count = code.shape[0] // 4
        want, plane = wanted(out.shape[0], capacity)
        for k in range(4):
            row = code[k * count : (k + 1) * count].T[:1].astype(jnp.int32)
            hit = (row == want) & (plane == k)
            placing[:, k * count : (k + 1) * count] = hit.astype(BF16)

    stacked = jnp.concatenate([piece[...] for piece in pieces], axis=0)
    out[...] = dot(placing[...], stacked).astype(BF16)


def gate_up_kernel(begins, last, *refs):
    pieces, (gate_o, gate_p, up_o, up_p, first) = refs[:5], refs[5:10]
    refs = refs[10:]
    if not begins:
        prev, refs = refs[:3], refs[3:]
    if last:
        (gb_o, gb_p, da_o, da_p), refs = refs[:4], refs[4:]
        (hidden_ref, factor_ref, low_ref, sums_ref), refs = refs[:4], refs[4:]
    gate, up, low = refs
    step = pl.program_id(0)
    units = gate_o.shape[1]

    @pl.when(step == 0)
    def _():
        for i, total in enumerate((gate, up, low)):
            total[...] = jnp.zeros_like(total) if begins else prev[i][...]

    rows = jnp.concatenate([piece[...] for piece in pieces], axis=0)
    gate[:, :units] += dot(rows, gate_o[...])
    gate[:, units:] += dot(rows, gate_p[...])
    up[:, :units] += dot(rows, up_o[...])
    up[:, units:] += dot(rows, up_p[...])
    low[...] += contract_last(rows, first[...])

    if last:

        @pl.when(step == pl.num_programs(0) - 1)
        def _():
            lowrank_in = low[...].astype(BF16)
            low_ref[...] = lowrank_in
            gate[:, :units] += dot(lowrank_in, gb_o[...])
            gate[:, units:] += dot(lowrank_in, gb_p[...])
            block = 32

            def some(i, carry):
                at = pl.ds(pl.multiple_of(i * block, block), block)
                gate_pre, up_pre = gate[at, :], up[at, :]
                sigmoid_val = jax.nn.sigmoid(gate_pre)
                slope = up_pre * sigmoid_val
                hidden_ref[at, :] = (gate_pre * slope).astype(BF16)
                factor_ref[at, :] = slope * (1.0 + gate_pre * (1.0 - sigmoid_val))
                return carry

            lax.fori_loop(0, gate.shape[0] // block, some, 0)
            sums_ref[...] = contract_last(da_o[...], hidden_ref[:, :units]) + contract_last(
                da_p[...], hidden_ref[:, units:]
            )


def halves(value):
    high = value.astype(BF16)
    return high, (value - high.astype(F32)).astype(BF16)


def raw_kernel(capacity, got_ref, down_o, down_p, first, total_ref, low_ref, total, low):
    units = down_o.shape[0]
    step = pl.program_id(0)

    @pl.when(step == 0)
    def _():
        total[...] = jnp.zeros_like(total)
        low[...] = jnp.zeros_like(low)

    rows = got_ref[...]
    total[:, :units] += contract_last(rows, down_o[...])
    total[:, units:] += contract_last(rows, down_p[...])
    low[...] += contract_last(rows, first[...])

    @pl.when(step == pl.num_programs(0) - 1)
    def _():
        order = order_of(total.shape[0], capacity)
        for source, out in ((total, total_ref), (low, low_ref)):
            high_part, low_part = halves(source[...])
            out[...] = dot(order, high_part) + dot(order, low_part)


def back_kernel(last, pieces, *refs):
    refs = list(refs)

    def take(number):
        taken = refs[:number]
        del refs[:number]
        return taken

    rows_refs, (down_o, down_p, first) = take(pieces), take(3)
    prev, (factor_ref, hidden_ref, low_in_ref) = take(2), take(3)
    gb_o, gb_p, da_o, da_p = take(4)
    if last:
        sums_before, *grads_before = take(3)
    sums_ref, grads_o_ref, grads_p_ref, total, low = refs
    step = pl.program_id(0)
    units = down_o.shape[0]

    @pl.when(step == 0)
    def _():
        total[...] = prev[0][...]
        low[...] = prev[1][...]

    rows = jnp.concatenate([piece[...] for piece in rows_refs], axis=0)
    total[:, :units] += contract_last(rows, down_o[...])
    total[:, units:] += contract_last(rows, down_p[...])
    low[...] += contract_last(rows, first[...])

    @pl.when(step == pl.num_programs(0) - 1)
    def _():
        lowrank_back = low[...].astype(BF16)
        rank = lowrank_back.shape[1]
        total_o = total[:, :units] + dot(lowrank_back, da_o[...])
        grad_o = (total_o * factor_ref[:, :units]).astype(BF16)
        total_p = total[:, units:] + dot(lowrank_back, da_p[...])
        grad_p = (total_p * factor_ref[:, units:]).astype(BF16)
        lowrank_in = low_in_ref[...]
        sums = contract_last(gb_o[...], grad_o) + contract_last(gb_p[...], grad_p)
        grads_o = contract_first(lowrank_in, grad_o)
        grads_p = contract_first(lowrank_in, grad_p)
        grads_b = contract_first(lowrank_back, hidden_ref[...])
        if last:
            done = sums_before.shape[1]
            sums_ref[:, :done] = sums_before[...]
            sums_ref[:, done:] = sums
        else:
            sums_ref[...] = sums
        for i, (out, top) in enumerate(((grads_o_ref, grads_o), (grads_p_ref, grads_p))):
            bottom = grads_b[:, i * units : (i + 1) * units]
            if last:
                top = top + grads_before[i][:rank, :]
                bottom = bottom + grads_before[i][rank:, :]
            out[:rank, :] = top
            out[rank:, :] = bottom


def select_kernel(counts, me_ref, *refs):
    number = sum(sum(side) for side in counts)
    ins, outs, sems = list(refs[:number]), refs[number:-1], refs[-1]
    sides = [[[ins.pop(0) for _ in range(pieces)] for pieces in side] for side in counts]
    span = outs[0].shape[1]
    plane = lax.div(me_ref[0], 2)

    def copies(which):
        found = []
        begin, end = which * span, (which + 1) * span
        for chunks, out in zip(sides, outs):
            base = 0
            for pieces in chunks:
                size = pieces[0].shape[1]
                low, high = max(begin, base), min(end, base + size)
                at = 0
                for piece in pieces:
                    rows = piece.shape[0]
                    if low < high:
                        found.append(
                            pltpu.make_async_copy(
                                piece.at[:, pl.ds(low - base, high - low)],
                                out.at[pl.ds(at, rows), pl.ds(low - begin, high - low)],
                                sems.at[len(found)],
                            )
                        )
                    at += rows
                base += size
        return found

    for which in range(4):

        @pl.when(plane == which)
        def _():
            found = copies(which)
            for copy in found:
                copy.start()
            for copy in found:
                copy.wait()


def product_kernel(rest, capacity, me_ref, tok_ref, cot_ref, *refs):
    mine_ref, theirs_ref = refs[-2:]
    rank, span = mine_ref.shape[1], tok_ref.shape[1]
    slots = tok_ref.shape[0] // 4
    me = me_ref[0]
    totals = []
    for own, *others in (refs[:4], refs[4:8]):
        total = own[...]
        for other, order in zip(others, ((2, 0, 3, 1), (1, 3, 0, 2), (3, 2, 1, 0))):
            value = other[...]
            total = total + jnp.concatenate(
                [value[:, i * slots : (i + 1) * slots] for i in order], axis=1
            )
        totals.append(total)
    half = span // 2
    even = lax.rem(me, 2) == 0
    crossed = lax.broadcasted_iota(jnp.int32, (rank, span), 1) + lax.div(me, 2) * span >= rest
    for side, rows_ref in enumerate((tok_ref, cot_ref)):
        both = jnp.concatenate(halves(totals[side]), axis=0)
        rows = rows_ref[...]
        if side == 1:
            both = jnp.concatenate([both, dot(both, order_of(rows.shape[0], capacity)).astype(BF16)], axis=0)
        wide = dot(both, rows)
        if side == 1:
            moved = wide[2 * rank : 3 * rank] + wide[3 * rank :]
        wide = wide[:rank] + wide[rank : 2 * rank]
        if side == 1:
            wide = jnp.where(crossed, moved, wide)
        mine_ref[side] = jnp.where(even, wide[:, :half], wide[:, half:])
        theirs_ref[side] = jnp.where(even, wide[:, half:], wide[:, :half])


def final_kernel(own_ref, other_ref, grads_ref, more_ref, ga_ref, gb_ref, da_ref, db_ref):
    rank = ga_ref.shape[1]
    ga_ref[0] = own_ref[0] + other_ref[0]
    db_ref[0] = own_ref[1] + other_ref[1]
    gb_ref[0] = grads_ref[:rank, :] + more_ref[:rank, :]
    da_ref[0] = grads_ref[rank:, :] + more_ref[rank:, :]


def body(
    tokens,
    cotangent,
    chosen_expert_index,
    router_weight,
    frozen_gate_weight,
    frozen_up_weight,
    frozen_down_weight,
    gate_adapter_first,
    gate_adapter_second,
    down_adapter_first,
    down_adapter_second,
):
    tie = lax.optimization_barrier
    experts = lax.axis_size("dp")
    count, top = chosen_expert_index.shape
    width = tokens.shape[1]
    first = width // UNIT * FIRST // 7 * UNIT
    spans = ((0, first), (first, width - first))
    rest, late = first, width - first
    capacity = 5 * count * top // (4 * experts)
    slots = experts * capacity
    every = 4 * slots
    gate_w, up_w, down_w = frozen_gate_weight[0], frozen_up_weight[0], frozen_down_weight[0]
    gate_a, gate_b = gate_adapter_first[0], gate_adapter_second[0]
    down_a, down_b = down_adapter_first[0], down_adapter_second[0]
    rank, units = gate_b.shape

    code = call(
        functools.partial(code_kernel, experts, capacity), shape((1, count), jnp.int32), 16, moved=1024
    )(chosen_expert_index.reshape(1, count))
    scaled, raw = call(
        scale_kernel,
        (shape((count, rest), BF16), shape((count, late + LANES), BF16)),
        VMEM_MIB,
        moved=4 * count * width,
    )(cotangent, router_weight.reshape(1, count), code)
    raw_steps = first_step(raw)

    def pack(code, *sources):
        spans = [(first, size) for _, first, size in sources]
        part = sum(size for _, size in spans) // PIECES
        return call(
            functools.partial(pack_kernel, spans, capacity),
            shape((every, part), BF16),
            32,
            flops=2 * every * PIECES * count * part,
            moved=2 * (PIECES * count + every) * part,
            grid=(1,),
            in_specs=[whole(1, count)]
            + [whole(*rows.shape) for rows, _, _ in sources],
            out_specs=whole(every, part),
        )(code, *[rows for rows, _, _ in sources])

    def across_dp(packed):
        sent = packed.reshape(experts, -1, packed.shape[1])
        return lax.all_to_all(sent, "dp", split_axis=0, concat_axis=0, tiled=True).reshape(packed.shape)

    def unpack(got, *sizes):
        return call(
            functools.partial(unpack_kernel, capacity),
            tuple(shape((slots, size), BF16) for size in sizes),
            VMEM_MIB,
            flops=2 * every * every * got.shape[1] // COVER,
            moved=4 * every * got.shape[1] // COVER,
        )(got)

    mine = (gate_w, up_w, down_w, jnp.concatenate([gate_b, down_a], axis=0))
    got = across_dp(pack(code, (tokens, *spans[0])))
    code, raw_steps = tie((code, raw_steps))
    raw_far = second_step(*raw_steps)
    sent = pack(code, (tokens, *spans[1]), (scaled, 0, rest))
    got, sent = tie((got, sent))
    (rows_0,) = unpack(got, first)
    rows_0, sent = tie((rows_0, sent))
    steps_0 = first_step(rows_0)
    got = across_dp(sent)
    raw_far, steps_0 = tie((raw_far, steps_0))
    far_0 = second_step(*steps_0)

    raw_pieces = (raw, *raw_steps, *raw_far)
    wide = late // PIECES
    packed_raw = call(
        functools.partial(pack_raw_kernel, capacity),
        shape((every, late), BF16),
        VMEM_MIB,
        flops=2 * every * 4 * count * late,
        moved=2 * (4 * count + every) * late,
        grid=(PIECES,),
        in_specs=[pl.BlockSpec((piece.shape[0], wide), lambda i: (0, i)) for piece in raw_pieces]
        + [
            pl.BlockSpec((piece.shape[0], LANES), lambda i: (0, late // LANES))
            for piece in raw_pieces
        ],
        out_specs=pl.BlockSpec((every, wide), lambda i: (0, i)),
        scratch_shapes=[pltpu.VMEM((every, 4 * count), BF16)],
    )(*raw_pieces, *raw_pieces)
    got, theirs, packed_raw = tie((got, tuple(swap_core(w) for w in mine), packed_raw))
    gate_p, up_p, down_p, small_p = theirs
    small = (gate_b, small_p[:rank], down_a, small_p[rank:])
    rows_1, rows_2 = unpack(got, width - first, rest)

    def piece_specs(pieces, depth):
        return [pl.BlockSpec((piece.shape[0], depth), lambda i: (0, i)) for piece in pieces]

    def tall(depth, first):
        return pl.BlockSpec((depth, units), lambda i: (first // depth + i, 0))

    def flat(rows, depth, first):
        return pl.BlockSpec((rows, depth), lambda i: (0, first // depth + i))

    totals = (shape((every, 2 * units), F32), shape((every, 2 * units), F32), shape((every, rank), F32))
    scratch = [pltpu.VMEM(s.shape, s.dtype) for s in totals]
    def gate_up(chunk, pieces, before):
        begins, last = chunk == 0, chunk == len(spans) - 1
        first, size = spans[chunk]
        depth = math.gcd(first, size) if first else size // 2
        outs = totals
        if last:
            outs = (
                shape((every, 2 * units), BF16),
                totals[0],
                shape((every, rank), BF16),
                shape((rank, every), F32),
            )
        extra = (before if before else ()) + (small if last else ())
        return call(
            functools.partial(gate_up_kernel, begins, last),
            outs,
            VMEM_MIB,
            flops=2 * every * size * 4 * units,
            moved=2 * size * (every + 4 * units),
            grid=(size // depth,),
            in_specs=piece_specs(pieces, depth)
            + [tall(depth, first)] * 4
            + [flat(rank, depth, first)]
            + [whole(*value.shape) for value in extra],
            out_specs=tuple(whole(*s.shape) for s in outs),
            scratch_shapes=scratch if last else [],
        )(*pieces, gate_w, gate_p, up_w, up_p, gate_a, *extra)

    rows_1, far_0 = tie((rows_1, far_0))
    got_raw = across_dp(packed_raw)
    steps_1 = first_step(rows_1)
    pieces_0 = (rows_0, *steps_0, *far_0)
    part_0 = gate_up(0, pieces_0, None)
    steps_1, part_0 = tie((steps_1, part_0))
    halves_1 = split_rows(*steps_1)
    halves_1, rows_2 = tie((halves_1, rows_2))
    far_1 = forward(*halves_1)
    steps_2 = first_step(rows_2)
    pieces_1 = (rows_1, *steps_1, *far_1)
    hidden, factor, low_in, sums_back = gate_up(1, pieces_1, part_0)
    depth = math.gcd(rest, late)
    back_0, low_0 = call(
        functools.partial(raw_kernel, capacity),
        (totals[0], totals[2]),
        VMEM_MIB,
        flops=2 * every * late * 2 * units,
        moved=2 * late * (every + 2 * units),
        grid=(late // depth,),
        in_specs=[
            pl.BlockSpec((every, depth), lambda i: (0, i)),
            flat(units, depth, rest),
            flat(units, depth, rest),
            flat(rank, depth, rest),
        ],
        out_specs=(whole(every, 2 * units), whole(every, rank)),
        scratch_shapes=[scratch[0], scratch[2]],
    )(got_raw, down_w, down_p, down_b)
    sums_back = exchanged(sums_back)
    steps_2, hidden, back_0 = tie((steps_2, hidden, back_0))
    far_2 = second_step(*steps_2)

    def back(last, pieces, at, *before):
        rows = sum(piece.shape[0] for piece in pieces)

        def block(columns):
            return pl.BlockSpec((rows, columns), lambda i: (at // rows, 0))

        outs = (
            shape((rank, every if last else rows), F32),
            *[shape((2 * rank, units), F32)] * 2,
        )
        depth = rest // 2
        return call(
            functools.partial(back_kernel, last, len(pieces)),
            outs,
            24 if last else 44,
            flops=2 * rows * rest * 2 * units,
            moved=2 * rest * (rows + 2 * units),
            grid=(rest // depth,),
            in_specs=piece_specs(pieces, depth)
            + [flat(units, depth, 0)] * 2
            + [flat(rank, depth, 0)]
            + [block(2 * units), block(rank), block(2 * units), block(2 * units), block(rank)]
            + [whole(rank, units)] * 4
            + [whole(*value.shape) for value in before],
            out_specs=tuple(whole(*s.shape) for s in outs),
            scratch_shapes=[pltpu.VMEM((rows, 2 * units), F32), pltpu.VMEM((rows, rank), F32)],
        )(*pieces, down_w, down_p, down_b, back_0, low_0, factor, hidden, low_in, *small, *before)

    far_2, sums_back = tie((far_2, sums_back))
    pieces_2 = (rows_2, *steps_2, *far_2)
    near = back(False, pieces_2[:3], 0)
    sums, grads, for_other = back(True, pieces_2[3:], 3 * slots, *near)

    me = lax.axis_index("seq").astype(jnp.int32).reshape(1)
    share = width // lax.axis_size("seq")
    scalar = pl.BlockSpec(memory_space=pltpu.SMEM)
    chunks = (*pieces_0, *pieces_1, *pieces_2, got_raw)
    tok, cot = call(
        functools.partial(select_kernel, ((5, 5), (5, 1))),
        (pltpu.VMEM((every, 2 * share), BF16),) * 2,
        VMEM_MIB,
        moved=16 * every * share,
        in_specs=[scalar] + [pl.BlockSpec(memory_space=pl.ANY)] * len(chunks),
        out_specs=(pl.BlockSpec(memory_space=pltpu.VMEM),) * 2,
        scratch_shapes=[pltpu.SemaphoreType.DMA((len(chunks),))],
    )(me, *chunks)
    own, other = call(
        functools.partial(product_kernel, rest, capacity),
        (shape((2, rank, share), F32),) * 2,
        16,
        flops=8 * rank * every * share,
        moved=8 * every * share,
        in_specs=[scalar]
        + [pl.BlockSpec(memory_space=pltpu.VMEM)] * 2
        + [whole(rank, every)] * 8,
    )(me, tok, cot, *exchanged(sums), *sums_back)
    return tuple(
        call(
            final_kernel,
            (
                shape((1, rank, share), F32),
                shape((1, rank, units), F32),
                shape((1, rank, units), F32),
                shape((1, rank, share), F32),
            ),
            8,
            moved=24 * rank * share,
        )(own, swap_core(other), grads, swap_core(for_other))
    )


def solution(mesh):
    return jax.shard_map(
        body,
        mesh=mesh,
        in_specs=(
            P(("dp", "seq"), None),
            P(("dp", "seq"), None),
            P(("dp", "seq"), None),
            P(("dp", "seq"), None),
            P("dp", None, "seq"),
            P("dp", None, "seq"),
            P("dp", "seq", None),
            P("dp", None, None),
            P("dp", None, "seq"),
            P("dp", None, "seq"),
            P("dp", None, None),
        ),
        out_specs=(
            P("dp", None, "seq"),
            P("dp", None, "seq"),
            P("dp", None, "seq"),
            P("dp", None, "seq"),
        ),
        check_vma=False,
    )
```

```python
import functools
import math

import jax
import jax.numpy as jnp
from jax import lax
from jax.experimental import pallas as pl
from jax.experimental.pallas import tpu as pltpu
from jax.sharding import PartitionSpec as P

PIECES = 4
FIRST = 4
UNIT = 1024
LANES = 128
COVER = 8
MIB = 1 << 20
VMEM_MIB = 58
BF16, F32 = jnp.bfloat16, jnp.float32


def dot(left, right):
    return jnp.dot(left, right, preferred_element_type=F32)


def contract_last(left, right):
    return lax.dot_general(left, right, (((1,), (1,)), ((), ())), preferred_element_type=F32)


def contract_first(left, right):
    return lax.dot_general(left, right, (((0,), (0,)), ((), ())), preferred_element_type=F32)


def shift_y(value, step):
    size = lax.axis_size("seq")
    planes = size // 2
    pairs = [
        (y * 2 + c, ((y + step) % planes) * 2 + c) for y in range(planes) for c in range(2)
    ]
    return lax.ppermute(value, "seq", pairs)


def swap_core(value):
    size = lax.axis_size("seq")
    return lax.ppermute(value, "seq", [(i, i ^ 1) for i in range(size)])


def first_step(rows):
    return shift_y(rows, 1), shift_y(rows, -1)


def exchanged(value):
    far = shift_y(value, 2)
    return value, shift_y(value, 1), shift_y(value, -1), far


def split_kernel(before_ref, after_ref, low_ref, high_ref):
    low_ref[...] = before_ref[...]
    high_ref[...] = after_ref[...]


def split_rows(before, after):
    rows, columns = before.shape[0] // 2, before.shape[1]
    part = pl.BlockSpec((rows, columns), lambda i: (0, 0))
    return call(
        split_kernel,
        (shape((rows, columns), before.dtype),) * 2,
        16,
        moved=2 * before.size,
        grid=(1,),
        in_specs=[part, pl.BlockSpec((rows, columns), lambda i: (1, 0))],
        out_specs=(part,) * 2,
    )(before, after)


def forward(low, high):
    return shift_y(low, 1), shift_y(high, -1)


def second_step(before, after):
    return forward(*split_rows(before, after))


def shape(dims, dtype):
    return jax.ShapeDtypeStruct(dims, dtype)


def call(kernel, outs, mib, flops=0, moved=0, **rest):
    return pl.pallas_call(
        kernel,
        out_shape=outs,
        compiler_params=pltpu.CompilerParams(vmem_limit_bytes=mib * MIB),
        cost_estimate=pl.CostEstimate(flops=COVER * flops, bytes_accessed=COVER * moved, transcendentals=0),
        **rest,
    )


def whole(*dims):
    return pl.BlockSpec(dims, lambda *_: (0,) * len(dims))


def scale(weight_ref, cot_ref, out, size):
    count = weight_ref.shape[1]
    column = jnp.broadcast_to(weight_ref[...], (count, count)).T[:, :1]
    for at in range(0, size, 512):
        out[:, at : at + 512] = (cot_ref[:, at : at + 512].astype(F32) * column).astype(BF16)


def scale_kernel(cot_ref, weight_ref, out_ref):
    scale(weight_ref, cot_ref, out_ref, out_ref.shape[1])


def scale_raw_kernel(cot_ref, weight_ref, code_ref, raw_ref, buffer, sem):
    late = buffer.shape[1]
    copy = pltpu.make_async_copy(cot_ref.at[:, pl.ds(cot_ref.shape[1] - late, late)], buffer, sem)
    copy.start()
    copy.wait()
    scale(weight_ref, buffer, raw_ref, late)
    count = code_ref.shape[1]
    codes = jnp.broadcast_to(code_ref[...], (count, count)).astype(F32).T
    raw_ref[:, late:] = codes[:, : raw_ref.shape[1] - late].astype(BF16)


def index_parts(count, outer, inner):
    row = lax.broadcasted_iota(jnp.int32, (count, 1), 0).astype(F32)
    first = jnp.floor((row + 0.5) * (1.0 / (outer * inner)))
    row = row - first * (outer * inner)
    second = jnp.floor((row + 0.5) * (1.0 / inner))
    return [part.astype(jnp.int32) for part in (first, second, row - second * inner)]


def wanted(count, capacity):
    expert, piece, slot = index_parts(count, 4, capacity)
    return expert * capacity + slot, piece


def order_of(count, capacity):
    piece, source, slot = index_parts(count, count // (4 * capacity), capacity)
    came = source * (4 * capacity) + piece * capacity + slot
    return (lax.broadcasted_iota(jnp.int32, (count, count), 1) == came).astype(BF16)


def code_kernel(experts, capacity, ids_ref, code_ref):
    ids = ids_ref[...]
    count = ids.shape[1]
    onehot = (lax.broadcasted_iota(jnp.int32, (experts, count), 0) == ids).astype(F32)
    ahead = (
        lax.broadcasted_iota(jnp.int32, (count, count), 0)
        < lax.broadcasted_iota(jnp.int32, (count, count), 1)
    ).astype(BF16)
    earlier = dot(onehot.astype(BF16), ahead)
    slot = jnp.sum(earlier * onehot, axis=0, keepdims=True).astype(jnp.int32)
    code_ref[...] = ids * capacity + slot


def pack_kernel(spans, capacity, code_ref, *refs):
    out = refs[-1]
    want, piece = wanted(out.shape[0], capacity)
    hit = code_ref[...] == want
    placing = jnp.concatenate(
        [(hit & (piece == q)).astype(BF16) for q in range(PIECES)], axis=1
    )
    at = 0
    for rows, (first, size) in zip(refs, spans):
        part = size // PIECES
        stacked = jnp.concatenate(
            [rows[:, first + q * part : first + (q + 1) * part] for q in range(PIECES)], axis=0
        )
        out[:, at : at + part] = dot(placing, stacked).astype(BF16)
        at += part


def unpack_kernel(capacity, got_ref, *outs):
    count = got_ref.shape[0]
    take = order_of(count, capacity)
    rows = count // PIECES
    at = 0
    for out in outs:
        part = out.shape[1] // PIECES
        taken = dot(take, got_ref[:, at : at + part]).astype(BF16)
        for q in range(PIECES):
            out[:, q * part : (q + 1) * part] = taken[q * rows : (q + 1) * rows]
        at += part


def pack_raw_kernel(capacity, *refs):
    pieces, codes, out, placing = refs[:5], refs[5:10], refs[10], refs[11]

    @pl.when(pl.program_id(0) == 0)
    def _():
        code = jnp.concatenate([piece[...] for piece in codes], axis=0).astype(F32)
        count = code.shape[0] // 4
        want, plane = wanted(out.shape[0], capacity)
        for k in range(4):
            row = code[k * count : (k + 1) * count].T[:1].astype(jnp.int32)
            hit = (row == want) & (plane == k)
            placing[:, k * count : (k + 1) * count] = hit.astype(BF16)

    stacked = jnp.concatenate([piece[...] for piece in pieces], axis=0)
    out[...] = dot(placing[...], stacked).astype(BF16)


def gate_up_kernel(begins, last, *refs):
    pieces, (gate_o, gate_p, up_o, up_p, first) = refs[:5], refs[5:10]
    refs = refs[10:]
    if not begins:
        prev, refs = refs[:3], refs[3:]
    if last:
        (gb_o, gb_p, da_o, da_p), refs = refs[:4], refs[4:]
        (hidden_ref, factor_ref, low_ref, sums_ref), refs = refs[:4], refs[4:]
    gate, up, low = refs
    step = pl.program_id(0)
    units = gate_o.shape[1]

    @pl.when(step == 0)
    def _():
        for i, total in enumerate((gate, up, low)):
            total[...] = jnp.zeros_like(total) if begins else prev[i][...]

    rows = jnp.concatenate([piece[...] for piece in pieces], axis=0)
    gate[:, :units] += dot(rows, gate_o[...])
    gate[:, units:] += dot(rows, gate_p[...])
    up[:, :units] += dot(rows, up_o[...])
    up[:, units:] += dot(rows, up_p[...])
    low[...] += contract_last(rows, first[...])

    if last:

        @pl.when(step == pl.num_programs(0) - 1)
        def _():
            lowrank_in = low[...].astype(BF16)
            low_ref[...] = lowrank_in
            gate[:, :units] += dot(lowrank_in, gb_o[...])
            gate[:, units:] += dot(lowrank_in, gb_p[...])
            block = 32

            def some(i, carry):
                at = pl.ds(pl.multiple_of(i * block, block), block)
                gate_pre, up_pre = gate[at, :], up[at, :]
                sigmoid_val = jax.nn.sigmoid(gate_pre)
                slope = up_pre * sigmoid_val
                hidden_ref[at, :] = (gate_pre * slope).astype(BF16)
                factor_ref[at, :] = slope * (1.0 + gate_pre * (1.0 - sigmoid_val))
                return carry

            lax.fori_loop(0, gate.shape[0] // block, some, 0)
            sums_ref[...] = contract_last(da_o[...], hidden_ref[:, :units]) + contract_last(
                da_p[...], hidden_ref[:, units:]
            )


def halves(value):
    high = value.astype(BF16)
    return high, (value - high.astype(F32)).astype(BF16)


def raw_kernel(capacity, got_ref, down_o, down_p, first, total_ref, low_ref, total, low):
    units = down_o.shape[0]
    step = pl.program_id(0)

    @pl.when(step == 0)
    def _():
        total[...] = jnp.zeros_like(total)
        low[...] = jnp.zeros_like(low)

    rows = got_ref[...]
    total[:, :units] += contract_last(rows, down_o[...])
    total[:, units:] += contract_last(rows, down_p[...])
    low[...] += contract_last(rows, first[...])

    @pl.when(step == pl.num_programs(0) - 1)
    def _():
        order = order_of(total.shape[0], capacity)
        for source, out in ((total, total_ref), (low, low_ref)):
            high_part, low_part = halves(source[...])
            out[...] = dot(order, high_part) + dot(order, low_part)


def back_kernel(last, pieces, *refs):
    refs = list(refs)

    def take(number):
        taken = refs[:number]
        del refs[:number]
        return taken

    rows_refs, (down_o, down_p, first) = take(pieces), take(3)
    prev, (factor_ref, hidden_ref, low_in_ref) = take(2), take(3)
    gb_o, gb_p, da_o, da_p = take(4)
    if last:
        sums_before, *grads_before = take(3)
    sums_ref, grads_o_ref, grads_p_ref, total, low = refs
    step = pl.program_id(0)
    units = down_o.shape[0]

    @pl.when(step == 0)
    def _():
        total[...] = prev[0][...]
        low[...] = prev[1][...]

    rows = jnp.concatenate([piece[...] for piece in rows_refs], axis=0)
    total[:, :units] += contract_last(rows, down_o[...])
    total[:, units:] += contract_last(rows, down_p[...])
    low[...] += contract_last(rows, first[...])

    @pl.when(step == pl.num_programs(0) - 1)
    def _():
        lowrank_back = low[...].astype(BF16)
        rank = lowrank_back.shape[1]
        total_o = total[:, :units] + dot(lowrank_back, da_o[...])
        grad_o = (total_o * factor_ref[:, :units]).astype(BF16)
        total_p = total[:, units:] + dot(lowrank_back, da_p[...])
        grad_p = (total_p * factor_ref[:, units:]).astype(BF16)
        lowrank_in = low_in_ref[...]
        sums = contract_last(gb_o[...], grad_o) + contract_last(gb_p[...], grad_p)
        grads_o = contract_first(lowrank_in, grad_o)
        grads_p = contract_first(lowrank_in, grad_p)
        grads_b = contract_first(lowrank_back, hidden_ref[...])
        if last:
            done = sums_before.shape[1]
            sums_ref[:, :done] = sums_before[...]
            sums_ref[:, done:] = sums
        else:
            sums_ref[...] = sums
        for i, (out, top) in enumerate(((grads_o_ref, grads_o), (grads_p_ref, grads_p))):
            bottom = grads_b[:, i * units : (i + 1) * units]
            if last:
                top = top + grads_before[i][:rank, :]
                bottom = bottom + grads_before[i][rank:, :]
            out[:rank, :] = top
            out[rank:, :] = bottom


def select_kernel(counts, me_ref, *refs):
    number = sum(sum(side) for side in counts)
    ins, outs, sems = list(refs[:number]), refs[number:-1], refs[-1]
    sides = [[[ins.pop(0) for _ in range(pieces)] for pieces in side] for side in counts]
    span = outs[0].shape[1]
    plane = lax.div(me_ref[0], 2)

    def copies(which):
        found = []
        begin, end = which * span, (which + 1) * span
        for chunks, out in zip(sides, outs):
            base = 0
            for pieces in chunks:
                size = pieces[0].shape[1]
                low, high = max(begin, base), min(end, base + size)
                at = 0
                for piece in pieces:
                    rows = piece.shape[0]
                    if low < high:
                        found.append(
                            pltpu.make_async_copy(
                                piece.at[:, pl.ds(low - base, high - low)],
                                out.at[pl.ds(at, rows), pl.ds(low - begin, high - low)],
                                sems.at[len(found)],
                            )
                        )
                    at += rows
                base += size
        return found

    for which in range(4):

        @pl.when(plane == which)
        def _():
            found = copies(which)
            for copy in found:
                copy.start()
            for copy in found:
                copy.wait()


def product_kernel(rest, capacity, me_ref, tok_ref, cot_ref, *refs):
    mine_ref, theirs_ref = refs[-2:]
    rank, span = mine_ref.shape[1], tok_ref.shape[1]
    slots = tok_ref.shape[0] // 4
    me = me_ref[0]
    totals = []
    for own, *others in (refs[:4], refs[4:8]):
        total = own[...]
        for other, order in zip(others, ((2, 0, 3, 1), (1, 3, 0, 2), (3, 2, 1, 0))):
            value = other[...]
            total = total + jnp.concatenate(
                [value[:, i * slots : (i + 1) * slots] for i in order], axis=1
            )
        totals.append(total)
    half = span // 2
    even = lax.rem(me, 2) == 0
    crossed = lax.broadcasted_iota(jnp.int32, (rank, span), 1) + lax.div(me, 2) * span >= rest
    for side, rows_ref in enumerate((tok_ref, cot_ref)):
        both = jnp.concatenate(halves(totals[side]), axis=0)
        rows = rows_ref[...]
        if side == 1:
            both = jnp.concatenate([both, dot(both, order_of(rows.shape[0], capacity)).astype(BF16)], axis=0)
        wide = dot(both, rows)
        if side == 1:
            moved = wide[2 * rank : 3 * rank] + wide[3 * rank :]
        wide = wide[:rank] + wide[rank : 2 * rank]
        if side == 1:
            wide = jnp.where(crossed, moved, wide)
        mine_ref[side] = jnp.where(even, wide[:, :half], wide[:, half:])
        theirs_ref[side] = jnp.where(even, wide[:, half:], wide[:, :half])


def final_kernel(own_ref, other_ref, grads_ref, more_ref, ga_ref, gb_ref, da_ref, db_ref):
    rank = ga_ref.shape[1]
    ga_ref[0] = own_ref[0] + other_ref[0]
    db_ref[0] = own_ref[1] + other_ref[1]
    gb_ref[0] = grads_ref[:rank, :] + more_ref[:rank, :]
    da_ref[0] = grads_ref[rank:, :] + more_ref[rank:, :]


def body(
    tokens,
    cotangent,
    chosen_expert_index,
    router_weight,
    frozen_gate_weight,
    frozen_up_weight,
    frozen_down_weight,
    gate_adapter_first,
    gate_adapter_second,
    down_adapter_first,
    down_adapter_second,
):
    tie = lax.optimization_barrier
    experts = lax.axis_size("dp")
    count, top = chosen_expert_index.shape
    width = tokens.shape[1]
    first = width // UNIT * FIRST // 7 * UNIT
    spans = ((0, first), (first, width - first))
    rest, late = first, width - first
    capacity = 5 * count * top // (4 * experts)
    slots = experts * capacity
    every = 4 * slots
    gate_w, up_w, down_w = frozen_gate_weight[0], frozen_up_weight[0], frozen_down_weight[0]
    gate_a, gate_b = gate_adapter_first[0], gate_adapter_second[0]
    down_a, down_b = down_adapter_first[0], down_adapter_second[0]
    rank, units = gate_b.shape

    code = call(
        functools.partial(code_kernel, experts, capacity), shape((1, count), jnp.int32), 16, moved=1024
    )(chosen_expert_index.reshape(1, count))
    weight = router_weight.reshape(1, count)
    raw = call(
        scale_raw_kernel,
        shape((count, late + LANES), BF16),
        VMEM_MIB,
        moved=4 * count * late,
        in_specs=[pl.BlockSpec(memory_space=pl.ANY), whole(1, count), whole(1, count)],
        scratch_shapes=[pltpu.VMEM((count, late), BF16), pltpu.SemaphoreType.DMA],
    )(cotangent, weight, code)
    scaled = call(
        scale_kernel,
        shape((count, rest), BF16),
        VMEM_MIB,
        moved=4 * count * rest,
        grid=(1,),
        in_specs=[pl.BlockSpec((count, rest), lambda i: (0, 0)), whole(1, count)],
        out_specs=whole(count, rest),
    )(cotangent, weight)
    raw_steps = first_step(raw)

    def pack(code, *sources):
        spans = [(first, size) for _, first, size in sources]
        part = sum(size for _, size in spans) // PIECES
        return call(
            functools.partial(pack_kernel, spans, capacity),
            shape((every, part), BF16),
            32,
            flops=2 * every * PIECES * count * part,
            moved=2 * (PIECES * count + every) * part,
            grid=(1,),
            in_specs=[whole(1, count)]
            + [whole(*rows.shape) for rows, _, _ in sources],
            out_specs=whole(every, part),
        )(code, *[rows for rows, _, _ in sources])

    def across_dp(packed):
        sent = packed.reshape(experts, -1, packed.shape[1])
        return lax.all_to_all(sent, "dp", split_axis=0, concat_axis=0, tiled=True).reshape(packed.shape)

    def unpack(got, *sizes):
        return call(
            functools.partial(unpack_kernel, capacity),
            tuple(shape((slots, size), BF16) for size in sizes),
            24 if len(sizes) == 1 else VMEM_MIB,
            flops=2 * every * every * got.shape[1] // COVER,
            moved=4 * every * got.shape[1] // COVER,
        )(got)

    mine = (gate_w, up_w, down_w, jnp.concatenate([gate_b, down_a], axis=0))
    got = across_dp(pack(code, (tokens, *spans[0])))
    code, raw_steps = tie((code, raw_steps))
    raw_far = second_step(*raw_steps)
    sent = pack(code, (tokens, *spans[1]), (scaled, 0, rest))
    got, sent = tie((got, sent))
    (rows_0,) = unpack(got, first)
    rows_0, sent = tie((rows_0, sent))
    steps_0 = first_step(rows_0)
    got = across_dp(sent)
    raw_far, steps_0 = tie((raw_far, steps_0))
    far_0 = second_step(*steps_0)

    raw_pieces = (raw, *raw_steps, *raw_far)
    wide = late // PIECES
    packed_raw = call(
        functools.partial(pack_raw_kernel, capacity),
        shape((every, late), BF16),
        VMEM_MIB,
        flops=2 * every * 4 * count * late,
        moved=2 * (4 * count + every) * late,
        grid=(PIECES,),
        in_specs=[pl.BlockSpec((piece.shape[0], wide), lambda i: (0, i)) for piece in raw_pieces]
        + [
            pl.BlockSpec((piece.shape[0], LANES), lambda i: (0, late // LANES))
            for piece in raw_pieces
        ],
        out_specs=pl.BlockSpec((every, wide), lambda i: (0, i)),
        scratch_shapes=[pltpu.VMEM((every, 4 * count), BF16)],
    )(*raw_pieces, *raw_pieces)
    got, theirs, packed_raw = tie((got, tuple(swap_core(w) for w in mine), packed_raw))
    gate_p, up_p, down_p, small_p = theirs
    small = (gate_b, small_p[:rank], down_a, small_p[rank:])
    rows_1, rows_2 = unpack(got, width - first, rest)

    def piece_specs(pieces, depth):
        return [pl.BlockSpec((piece.shape[0], depth), lambda i: (0, i)) for piece in pieces]

    def tall(depth, first):
        return pl.BlockSpec((depth, units), lambda i: (first // depth + i, 0))

    def flat(rows, depth, first):
        return pl.BlockSpec((rows, depth), lambda i: (0, first // depth + i))

    totals = (shape((every, 2 * units), F32), shape((every, 2 * units), F32), shape((every, rank), F32))
    scratch = [pltpu.VMEM(s.shape, s.dtype) for s in totals]
    def gate_up(chunk, pieces, before):
        begins, last = chunk == 0, chunk == len(spans) - 1
        first, size = spans[chunk]
        depth = math.gcd(first, size) if first else size // 2
        outs = totals
        if last:
            outs = (
                shape((every, 2 * units), BF16),
                totals[0],
                shape((every, rank), BF16),
                shape((rank, every), F32),
            )
        extra = (before if before else ()) + (small if last else ())
        return call(
            functools.partial(gate_up_kernel, begins, last),
            outs,
            VMEM_MIB,
            flops=2 * every * size * 4 * units,
            moved=2 * size * (every + 4 * units),
            grid=(size // depth,),
            in_specs=piece_specs(pieces, depth)
            + [tall(depth, first)] * 4
            + [flat(rank, depth, first)]
            + [whole(*value.shape) for value in extra],
            out_specs=tuple(whole(*s.shape) for s in outs),
            scratch_shapes=scratch if last else [],
        )(*pieces, gate_w, gate_p, up_w, up_p, gate_a, *extra)

    rows_1, far_0 = tie((rows_1, far_0))
    got_raw = across_dp(packed_raw)
    steps_1 = first_step(rows_1)
    pieces_0 = (rows_0, *steps_0, *far_0)
    part_0 = gate_up(0, pieces_0, None)
    steps_1, part_0 = tie((steps_1, part_0))
    halves_1 = split_rows(*steps_1)
    halves_1, rows_2 = tie((halves_1, rows_2))
    far_1 = forward(*halves_1)
    steps_2 = first_step(rows_2)
    pieces_1 = (rows_1, *steps_1, *far_1)
    hidden, factor, low_in, sums_back = gate_up(1, pieces_1, part_0)
    depth = math.gcd(rest, late)
    back_0, low_0 = call(
        functools.partial(raw_kernel, capacity),
        (totals[0], totals[2]),
        VMEM_MIB,
        flops=2 * every * late * 2 * units,
        moved=2 * late * (every + 2 * units),
        grid=(late // depth,),
        in_specs=[
            pl.BlockSpec((every, depth), lambda i: (0, i)),
            flat(units, depth, rest),
            flat(units, depth, rest),
            flat(rank, depth, rest),
        ],
        out_specs=(whole(every, 2 * units), whole(every, rank)),
        scratch_shapes=[scratch[0], scratch[2]],
    )(got_raw, down_w, down_p, down_b)
    sums_back = exchanged(sums_back)
    steps_2, hidden, back_0 = tie((steps_2, hidden, back_0))
    far_2 = second_step(*steps_2)

    def back(last, pieces, at, *before):
        rows = sum(piece.shape[0] for piece in pieces)

        def block(columns):
            return pl.BlockSpec((rows, columns), lambda i: (at // rows, 0))

        outs = (
            shape((rank, every if last else rows), F32),
            *[shape((2 * rank, units), F32)] * 2,
        )
        depth = rest // 2
        return call(
            functools.partial(back_kernel, last, len(pieces)),
            outs,
            24 if last else 44,
            flops=2 * rows * rest * 2 * units,
            moved=2 * rest * (rows + 2 * units),
            grid=(rest // depth,),
            in_specs=piece_specs(pieces, depth)
            + [flat(units, depth, 0)] * 2
            + [flat(rank, depth, 0)]
            + [block(2 * units), block(rank), block(2 * units), block(2 * units), block(rank)]
            + [whole(rank, units)] * 4
            + [whole(*value.shape) for value in before],
            out_specs=tuple(whole(*s.shape) for s in outs),
            scratch_shapes=[pltpu.VMEM((rows, 2 * units), F32), pltpu.VMEM((rows, rank), F32)],
        )(*pieces, down_w, down_p, down_b, back_0, low_0, factor, hidden, low_in, *small, *before)

    far_2, sums_back = tie((far_2, sums_back))
    pieces_2 = (rows_2, *steps_2, *far_2)
    near = back(False, pieces_2[:3], 0)
    sums, grads, for_other = back(True, pieces_2[3:], 3 * slots, *near)

    me = lax.axis_index("seq").astype(jnp.int32).reshape(1)
    share = width // lax.axis_size("seq")
    scalar = pl.BlockSpec(memory_space=pltpu.SMEM)
    chunks = (*pieces_0, *pieces_1, *pieces_2, got_raw)
    tok, cot = call(
        functools.partial(select_kernel, ((5, 5), (5, 1))),
        (pltpu.VMEM((every, 2 * share), BF16),) * 2,
        VMEM_MIB,
        moved=16 * every * share,
        in_specs=[scalar] + [pl.BlockSpec(memory_space=pl.ANY)] * len(chunks),
        out_specs=(pl.BlockSpec(memory_space=pltpu.VMEM),) * 2,
        scratch_shapes=[pltpu.SemaphoreType.DMA((len(chunks),))],
    )(me, *chunks)
    own, other = call(
        functools.partial(product_kernel, rest, capacity),
        (shape((2, rank, share), F32),) * 2,
        16,
        flops=8 * rank * every * share,
        moved=8 * every * share,
        in_specs=[scalar]
        + [pl.BlockSpec(memory_space=pltpu.VMEM)] * 2
        + [whole(rank, every)] * 8,
    )(me, tok, cot, *exchanged(sums), *sums_back)
    return tuple(
        call(
            final_kernel,
            (
                shape((1, rank, share), F32),
                shape((1, rank, units), F32),
                shape((1, rank, units), F32),
                shape((1, rank, share), F32),
            ),
            8,
            moved=24 * rank * share,
        )(own, swap_core(other), grads, swap_core(for_other))
    )


def solution(mesh):
    return jax.shard_map(
        body,
        mesh=mesh,
        in_specs=(
            P(("dp", "seq"), None),
            P(("dp", "seq"), None),
            P(("dp", "seq"), None),
            P(("dp", "seq"), None),
            P("dp", None, "seq"),
            P("dp", None, "seq"),
            P("dp", "seq", None),
            P("dp", None, None),
            P("dp", None, "seq"),
            P("dp", None, "seq"),
            P("dp", None, None),
        ),
        out_specs=(
            P("dp", None, "seq"),
            P("dp", None, "seq"),
            P("dp", None, "seq"),
            P("dp", None, "seq"),
        ),
        check_vma=False,
    )
```

```python
import functools
import math

import jax
import jax.numpy as jnp
from jax import lax
from jax.experimental import pallas as pl
from jax.experimental.pallas import tpu as pltpu
from jax.sharding import PartitionSpec as P

PIECES = 4
FIRST = 4
UNIT = 1024
LANES = 128
COVER = 8
MIB = 1 << 20
VMEM_MIB = 58
BF16, F32 = jnp.bfloat16, jnp.float32


def dot(left, right):
    return jnp.dot(left, right, preferred_element_type=F32)


def contract_last(left, right):
    return lax.dot_general(left, right, (((1,), (1,)), ((), ())), preferred_element_type=F32)


def contract_first(left, right):
    return lax.dot_general(left, right, (((0,), (0,)), ((), ())), preferred_element_type=F32)


def shift_y(value, step):
    size = lax.axis_size("seq")
    planes = size // 2
    pairs = [
        (y * 2 + c, ((y + step) % planes) * 2 + c) for y in range(planes) for c in range(2)
    ]
    return lax.ppermute(value, "seq", pairs)


def swap_core(value):
    size = lax.axis_size("seq")
    return lax.ppermute(value, "seq", [(i, i ^ 1) for i in range(size)])


def first_step(rows):
    return shift_y(rows, 1), shift_y(rows, -1)


def exchanged(value):
    far = shift_y(value, 2)
    return value, shift_y(value, 1), shift_y(value, -1), far


def split_kernel(before_ref, after_ref, low_ref, high_ref):
    low_ref[...] = before_ref[...]
    high_ref[...] = after_ref[...]


def split_rows(before, after):
    rows, columns = before.shape[0] // 2, before.shape[1]
    part = pl.BlockSpec((rows, columns), lambda i: (0, 0))
    return call(
        split_kernel,
        (shape((rows, columns), before.dtype),) * 2,
        16,
        moved=2 * before.size,
        grid=(1,),
        in_specs=[part, pl.BlockSpec((rows, columns), lambda i: (1, 0))],
        out_specs=(part,) * 2,
    )(before, after)


def forward(low, high):
    return shift_y(low, 1), shift_y(high, -1)


def second_step(before, after):
    return forward(*split_rows(before, after))


def shape(dims, dtype):
    return jax.ShapeDtypeStruct(dims, dtype)


def call(kernel, outs, mib, flops=0, moved=0, **rest):
    return pl.pallas_call(
        kernel,
        out_shape=outs,
        compiler_params=pltpu.CompilerParams(vmem_limit_bytes=mib * MIB),
        cost_estimate=pl.CostEstimate(flops=COVER * flops, bytes_accessed=COVER * moved, transcendentals=0),
        **rest,
    )


def whole(*dims):
    return pl.BlockSpec(dims, lambda *_: (0,) * len(dims))


def scale(weight_ref, cot_ref, out, size):
    count = weight_ref.shape[1]
    column = jnp.broadcast_to(weight_ref[...], (count, count)).T[:, :1]
    for at in range(0, size, 512):
        out[:, at : at + 512] = (cot_ref[:, at : at + 512].astype(F32) * column).astype(BF16)


def scale_kernel(cot_ref, weight_ref, out_ref):
    scale(weight_ref, cot_ref, out_ref, out_ref.shape[1])


def scale_raw_kernel(cot_ref, weight_ref, code_ref, raw_ref, buffer, sem):
    late = buffer.shape[1]
    copy = pltpu.make_async_copy(cot_ref.at[:, pl.ds(cot_ref.shape[1] - late, late)], buffer, sem)
    copy.start()
    copy.wait()
    scale(weight_ref, buffer, raw_ref, late)
    count = code_ref.shape[1]
    codes = jnp.broadcast_to(code_ref[...], (count, count)).astype(F32).T
    raw_ref[:, late:] = codes[:, : raw_ref.shape[1] - late].astype(BF16)


def index_parts(count, outer, inner):
    row = lax.broadcasted_iota(jnp.int32, (count, 1), 0).astype(F32)
    first = jnp.floor((row + 0.5) * (1.0 / (outer * inner)))
    row = row - first * (outer * inner)
    second = jnp.floor((row + 0.5) * (1.0 / inner))
    return [part.astype(jnp.int32) for part in (first, second, row - second * inner)]


def wanted(count, capacity):
    expert, piece, slot = index_parts(count, 4, capacity)
    return expert * capacity + slot, piece


def order_of(count, capacity):
    piece, source, slot = index_parts(count, count // (4 * capacity), capacity)
    came = source * (4 * capacity) + piece * capacity + slot
    return (lax.broadcasted_iota(jnp.int32, (count, count), 1) == came).astype(BF16)


def code_kernel(experts, capacity, ids_ref, code_ref):
    ids = ids_ref[...]
    count = ids.shape[1]
    onehot = (lax.broadcasted_iota(jnp.int32, (experts, count), 0) == ids).astype(F32)
    ahead = (
        lax.broadcasted_iota(jnp.int32, (count, count), 0)
        < lax.broadcasted_iota(jnp.int32, (count, count), 1)
    ).astype(BF16)
    earlier = dot(onehot.astype(BF16), ahead)
    slot = jnp.sum(earlier * onehot, axis=0, keepdims=True).astype(jnp.int32)
    code_ref[...] = ids * capacity + slot


def pack_kernel(spans, capacity, code_ref, *refs):
    out = refs[-1]
    want, piece = wanted(out.shape[0], capacity)
    hit = code_ref[...] == want
    placing = jnp.concatenate(
        [(hit & (piece == q)).astype(BF16) for q in range(PIECES)], axis=1
    )
    at = 0
    for rows, (first, size) in zip(refs, spans):
        part = size // PIECES
        stacked = jnp.concatenate(
            [rows[:, first + q * part : first + (q + 1) * part] for q in range(PIECES)], axis=0
        )
        out[:, at : at + part] = dot(placing, stacked).astype(BF16)
        at += part


def unpack_kernel(capacity, got_ref, *outs):
    count = got_ref.shape[0]
    take = order_of(count, capacity)
    rows = count // PIECES
    at = 0
    for out in outs:
        part = out.shape[1] // PIECES
        taken = dot(take, got_ref[:, at : at + part]).astype(BF16)
        for q in range(PIECES):
            out[:, q * part : (q + 1) * part] = taken[q * rows : (q + 1) * rows]
        at += part


def pack_raw_kernel(capacity, *refs):
    pieces, codes, out, placing = refs[:5], refs[5:10], refs[10], refs[11]

    @pl.when(pl.program_id(0) == 0)
    def _():
        code = jnp.concatenate([piece[...] for piece in codes], axis=0).astype(F32)
        count = code.shape[0] // 4
        want, plane = wanted(out.shape[0], capacity)
        for k in range(4):
            row = code[k * count : (k + 1) * count].T[:1].astype(jnp.int32)
            hit = (row == want) & (plane == k)
            placing[:, k * count : (k + 1) * count] = hit.astype(BF16)

    stacked = jnp.concatenate([piece[...] for piece in pieces], axis=0)
    out[...] = dot(placing[...], stacked).astype(BF16)


def gate_up_kernel(begins, last, *refs):
    pieces, (gate_o, gate_p, up_o, up_p, first) = refs[:5], refs[5:10]
    refs = refs[10:]
    if not begins:
        prev, refs = refs[:3], refs[3:]
    if last:
        (gb_o, gb_p, da_o, da_p), refs = refs[:4], refs[4:]
        (hidden_ref, factor_ref, low_ref, sums_ref), refs = refs[:4], refs[4:]
    gate, up, low = refs
    step = pl.program_id(0)
    units = gate_o.shape[1]

    @pl.when(step == 0)
    def _():
        for i, total in enumerate((gate, up, low)):
            total[...] = jnp.zeros_like(total) if begins else prev[i][...]

    rows = jnp.concatenate([piece[...] for piece in pieces], axis=0)
    gate[:, :units] += dot(rows, gate_o[...])
    gate[:, units:] += dot(rows, gate_p[...])
    up[:, :units] += dot(rows, up_o[...])
    up[:, units:] += dot(rows, up_p[...])
    low[...] += contract_last(rows, first[...])

    if last:

        @pl.when(step == pl.num_programs(0) - 1)
        def _():
            lowrank_in = low[...].astype(BF16)
            low_ref[...] = lowrank_in
            gate[:, :units] += dot(lowrank_in, gb_o[...])
            gate[:, units:] += dot(lowrank_in, gb_p[...])
            block = 32

            def some(i, carry):
                at = pl.ds(pl.multiple_of(i * block, block), block)
                gate_pre, up_pre = gate[at, :], up[at, :]
                sigmoid_val = jax.nn.sigmoid(gate_pre)
                slope = up_pre * sigmoid_val
                hidden_ref[at, :] = (gate_pre * slope).astype(BF16)
                factor_ref[at, :] = slope * (1.0 + gate_pre * (1.0 - sigmoid_val))
                return carry

            lax.fori_loop(0, gate.shape[0] // block, some, 0)
            sums_ref[...] = contract_last(da_o[...], hidden_ref[:, :units]) + contract_last(
                da_p[...], hidden_ref[:, units:]
            )


def halves(value):
    high = value.astype(BF16)
    return high, (value - high.astype(F32)).astype(BF16)


def raw_kernel(capacity, got_ref, down_o, down_p, first, total_ref, low_ref, total, low):
    units = down_o.shape[0]
    step = pl.program_id(0)

    @pl.when(step == 0)
    def _():
        total[...] = jnp.zeros_like(total)
        low[...] = jnp.zeros_like(low)

    rows = got_ref[...]
    total[:, :units] += contract_last(rows, down_o[...])
    total[:, units:] += contract_last(rows, down_p[...])
    low[...] += contract_last(rows, first[...])

    @pl.when(step == pl.num_programs(0) - 1)
    def _():
        order = order_of(total.shape[0], capacity)
        for source, out in ((total, total_ref), (low, low_ref)):
            high_part, low_part = halves(source[...])
            out[...] = dot(order, high_part) + dot(order, low_part)


def back_kernel(last, pieces, *refs):
    refs = list(refs)

    def take(number):
        taken = refs[:number]
        del refs[:number]
        return taken

    rows_refs, (down_o, down_p, first) = take(pieces), take(3)
    prev, (factor_ref, hidden_ref, low_in_ref) = take(2), take(3)
    gb_o, gb_p, da_o, da_p = take(4)
    if last:
        sums_before, *grads_before = take(3)
    sums_ref, grads_o_ref, grads_p_ref, total, low = refs
    step = pl.program_id(0)
    units = down_o.shape[0]

    @pl.when(step == 0)
    def _():
        total[...] = prev[0][...]
        low[...] = prev[1][...]

    rows = jnp.concatenate([piece[...] for piece in rows_refs], axis=0)
    total[:, :units] += contract_last(rows, down_o[...])
    total[:, units:] += contract_last(rows, down_p[...])
    low[...] += contract_last(rows, first[...])

    @pl.when(step == pl.num_programs(0) - 1)
    def _():
        lowrank_back = low[...].astype(BF16)
        rank = lowrank_back.shape[1]
        total_o = total[:, :units] + dot(lowrank_back, da_o[...])
        grad_o = (total_o * factor_ref[:, :units]).astype(BF16)
        total_p = total[:, units:] + dot(lowrank_back, da_p[...])
        grad_p = (total_p * factor_ref[:, units:]).astype(BF16)
        lowrank_in = low_in_ref[...]
        sums = contract_last(gb_o[...], grad_o) + contract_last(gb_p[...], grad_p)
        grads_o = contract_first(lowrank_in, grad_o)
        grads_p = contract_first(lowrank_in, grad_p)
        grads_b = contract_first(lowrank_back, hidden_ref[...])
        if last:
            done = sums_before.shape[1]
            sums_ref[:, :done] = sums_before[...]
            sums_ref[:, done:] = sums
        else:
            sums_ref[...] = sums
        for i, (out, top) in enumerate(((grads_o_ref, grads_o), (grads_p_ref, grads_p))):
            bottom = grads_b[:, i * units : (i + 1) * units]
            if last:
                top = top + grads_before[i][:rank, :]
                bottom = bottom + grads_before[i][rank:, :]
            out[:rank, :] = top
            out[rank:, :] = bottom


def select_kernel(counts, me_ref, *refs):
    number = sum(sum(side) for side in counts)
    ins, outs, sems = list(refs[:number]), refs[number:-1], refs[-1]
    sides = [[[ins.pop(0) for _ in range(pieces)] for pieces in side] for side in counts]
    span = outs[0].shape[1]
    plane = lax.div(me_ref[0], 2)

    def copies(which):
        found = []
        begin, end = which * span, (which + 1) * span
        for chunks, out in zip(sides, outs):
            base = 0
            for pieces in chunks:
                size = pieces[0].shape[1]
                low, high = max(begin, base), min(end, base + size)
                at = 0
                for piece in pieces:
                    rows = piece.shape[0]
                    if low < high:
                        found.append(
                            pltpu.make_async_copy(
                                piece.at[:, pl.ds(low - base, high - low)],
                                out.at[pl.ds(at, rows), pl.ds(low - begin, high - low)],
                                sems.at[len(found)],
                            )
                        )
                    at += rows
                base += size
        return found

    for which in range(4):

        @pl.when(plane == which)
        def _():
            found = copies(which)
            for copy in found:
                copy.start()
            for copy in found:
                copy.wait()


def product_kernel(rest, capacity, me_ref, tok_ref, cot_ref, *refs):
    mine_ref, theirs_ref = refs[-2:]
    rank, span = mine_ref.shape[1], tok_ref.shape[1]
    slots = tok_ref.shape[0] // 4
    me = me_ref[0]
    totals = []
    for own, *others in (refs[:4], refs[4:8]):
        total = own[...]
        for other, order in zip(others, ((2, 0, 3, 1), (1, 3, 0, 2), (3, 2, 1, 0))):
            value = other[...]
            total = total + jnp.concatenate(
                [value[:, i * slots : (i + 1) * slots] for i in order], axis=1
            )
        totals.append(total)
    half = span // 2
    even = lax.rem(me, 2) == 0
    crossed = lax.broadcasted_iota(jnp.int32, (rank, span), 1) + lax.div(me, 2) * span >= rest
    for side, rows_ref in enumerate((tok_ref, cot_ref)):
        both = jnp.concatenate(halves(totals[side]), axis=0)
        rows = rows_ref[...]
        if side == 1:
            both = jnp.concatenate([both, dot(both, order_of(rows.shape[0], capacity)).astype(BF16)], axis=0)
        wide = dot(both, rows)
        if side == 1:
            moved = wide[2 * rank : 3 * rank] + wide[3 * rank :]
        wide = wide[:rank] + wide[rank : 2 * rank]
        if side == 1:
            wide = jnp.where(crossed, moved, wide)
        mine_ref[side] = jnp.where(even, wide[:, :half], wide[:, half:])
        theirs_ref[side] = jnp.where(even, wide[:, half:], wide[:, :half])


def final_kernel(own_ref, other_ref, grads_ref, more_ref, ga_ref, gb_ref, da_ref, db_ref):
    rank = ga_ref.shape[1]
    ga_ref[0] = own_ref[0] + other_ref[0]
    db_ref[0] = own_ref[1] + other_ref[1]
    gb_ref[0] = grads_ref[:rank, :] + more_ref[:rank, :]
    da_ref[0] = grads_ref[rank:, :] + more_ref[rank:, :]


def body(
    tokens,
    cotangent,
    chosen_expert_index,
    router_weight,
    frozen_gate_weight,
    frozen_up_weight,
    frozen_down_weight,
    gate_adapter_first,
    gate_adapter_second,
    down_adapter_first,
    down_adapter_second,
):
    tie = lax.optimization_barrier
    experts = lax.axis_size("dp")
    count, top = chosen_expert_index.shape
    width = tokens.shape[1]
    first = width // UNIT * FIRST // 7 * UNIT
    spans = ((0, first), (first, width - first))
    rest, late = first, width - first
    capacity = 5 * count * top // (4 * experts)
    slots = experts * capacity
    every = 4 * slots
    gate_w, up_w, down_w = frozen_gate_weight[0], frozen_up_weight[0], frozen_down_weight[0]
    gate_a, gate_b = gate_adapter_first[0], gate_adapter_second[0]
    down_a, down_b = down_adapter_first[0], down_adapter_second[0]
    rank, units = gate_b.shape

    code = call(
        functools.partial(code_kernel, experts, capacity), shape((1, count), jnp.int32), 16, moved=1024
    )(chosen_expert_index.reshape(1, count))
    weight = router_weight.reshape(1, count)
    raw = call(
        scale_raw_kernel,
        shape((count, late + LANES), BF16),
        VMEM_MIB,
        moved=4 * count * late,
        in_specs=[pl.BlockSpec(memory_space=pl.ANY), whole(1, count), whole(1, count)],
        scratch_shapes=[pltpu.VMEM((count, late), BF16), pltpu.SemaphoreType.DMA],
    )(cotangent, weight, code)
    scaled = call(
        scale_kernel,
        shape((count, rest), BF16),
        VMEM_MIB,
        moved=4 * count * rest,
        grid=(1,),
        in_specs=[pl.BlockSpec((count, rest), lambda i: (0, 0)), whole(1, count)],
        out_specs=whole(count, rest),
    )(cotangent, weight)
    raw_steps = first_step(raw)

    def pack(code, *sources):
        spans = [(first, size) for _, first, size in sources]
        part = sum(size for _, size in spans) // PIECES
        return call(
            functools.partial(pack_kernel, spans, capacity),
            shape((every, part), BF16),
            32,
            flops=2 * every * PIECES * count * part,
            moved=2 * (PIECES * count + every) * part,
            grid=(1,),
            in_specs=[whole(1, count)]
            + [whole(*rows.shape) for rows, _, _ in sources],
            out_specs=whole(every, part),
        )(code, *[rows for rows, _, _ in sources])

    def across_dp(packed):
        sent = packed.reshape(experts, -1, packed.shape[1])
        return lax.all_to_all(sent, "dp", split_axis=0, concat_axis=0, tiled=True).reshape(packed.shape)

    def unpack(got, *sizes):
        return call(
            functools.partial(unpack_kernel, capacity),
            tuple(shape((slots, size), BF16) for size in sizes),
            24 if len(sizes) == 1 else VMEM_MIB,
            flops=2 * every * every * got.shape[1] // COVER,
            moved=4 * every * got.shape[1] // COVER,
        )(got)

    mine = (gate_w, up_w, down_w, jnp.concatenate([gate_b, down_a], axis=0))
    got = across_dp(pack(code, (tokens, *spans[0])))
    code, raw_steps = tie((code, raw_steps))
    raw_far = second_step(*raw_steps)
    sent = pack(code, (tokens, *spans[1]), (scaled, 0, rest))
    got, sent = tie((got, sent))
    (rows_0,) = unpack(got, first)
    rows_0, sent = tie((rows_0, sent))
    steps_0 = first_step(rows_0)
    got = across_dp(sent)
    raw_far, steps_0 = tie((raw_far, steps_0))
    far_0 = second_step(*steps_0)

    raw_pieces = (raw, *raw_steps, *raw_far)
    wide = late // PIECES
    packed_raw = call(
        functools.partial(pack_raw_kernel, capacity),
        shape((every, late), BF16),
        VMEM_MIB,
        flops=2 * every * 4 * count * late,
        moved=2 * (4 * count + every) * late,
        grid=(PIECES,),
        in_specs=[pl.BlockSpec((piece.shape[0], wide), lambda i: (0, i)) for piece in raw_pieces]
        + [
            pl.BlockSpec((piece.shape[0], LANES), lambda i: (0, late // LANES))
            for piece in raw_pieces
        ],
        out_specs=pl.BlockSpec((every, wide), lambda i: (0, i)),
        scratch_shapes=[pltpu.VMEM((every, 4 * count), BF16)],
    )(*raw_pieces, *raw_pieces)
    got, theirs, packed_raw = tie((got, tuple(swap_core(w) for w in mine), packed_raw))
    gate_p, up_p, down_p, small_p = theirs
    small = (gate_b, small_p[:rank], down_a, small_p[rank:])
    rows_1, rows_2 = unpack(got, width - first, rest)

    def piece_specs(pieces, depth):
        return [pl.BlockSpec((piece.shape[0], depth), lambda i: (0, i)) for piece in pieces]

    def tall(depth, first):
        return pl.BlockSpec((depth, units), lambda i: (first // depth + i, 0))

    def flat(rows, depth, first):
        return pl.BlockSpec((rows, depth), lambda i: (0, first // depth + i))

    totals = (shape((every, 2 * units), F32), shape((every, 2 * units), F32), shape((every, rank), F32))
    scratch = [pltpu.VMEM(s.shape, s.dtype) for s in totals]
    def gate_up(chunk, pieces, before):
        begins, last = chunk == 0, chunk == len(spans) - 1
        first, size = spans[chunk]
        depth = math.gcd(first, size) if first else size // 2
        outs = totals
        if last:
            outs = (
                shape((every, 2 * units), BF16),
                totals[0],
                shape((every, rank), BF16),
                shape((rank, every), F32),
            )
        extra = (before if before else ()) + (small if last else ())
        return call(
            functools.partial(gate_up_kernel, begins, last),
            outs,
            VMEM_MIB,
            flops=every * size * 3 * units,
            moved=2 * size * (every + 4 * units),
            grid=(size // depth,),
            in_specs=piece_specs(pieces, depth)
            + [tall(depth, first)] * 4
            + [flat(rank, depth, first)]
            + [whole(*value.shape) for value in extra],
            out_specs=tuple(whole(*s.shape) for s in outs),
            scratch_shapes=scratch if last else [],
        )(*pieces, gate_w, gate_p, up_w, up_p, gate_a, *extra)

    rows_1, far_0 = tie((rows_1, far_0))
    got_raw = across_dp(packed_raw)
    steps_1 = first_step(rows_1)
    pieces_0 = (rows_0, *steps_0, *far_0)
    part_0 = gate_up(0, pieces_0, None)
    steps_1, part_0 = tie((steps_1, part_0))
    halves_1 = split_rows(*steps_1)
    halves_1, rows_2 = tie((halves_1, rows_2))
    far_1 = forward(*halves_1)
    steps_2 = first_step(rows_2)
    pieces_1 = (rows_1, *steps_1, *far_1)
    hidden, factor, low_in, sums_back = gate_up(1, pieces_1, part_0)
    depth = math.gcd(rest, late)
    back_0, low_0 = call(
        functools.partial(raw_kernel, capacity),
        (totals[0], totals[2]),
        VMEM_MIB,
        flops=2 * every * late * 2 * units,
        moved=2 * late * (every + 2 * units),
        grid=(late // depth,),
        in_specs=[
            pl.BlockSpec((every, depth), lambda i: (0, i)),
            flat(units, depth, rest),
            flat(units, depth, rest),
            flat(rank, depth, rest),
        ],
        out_specs=(whole(every, 2 * units), whole(every, rank)),
        scratch_shapes=[scratch[0], scratch[2]],
    )(got_raw, down_w, down_p, down_b)
    sums_back = exchanged(sums_back)
    steps_2, hidden, back_0 = tie((steps_2, hidden, back_0))
    far_2 = second_step(*steps_2)

    def back(last, pieces, at, *before):
        rows = sum(piece.shape[0] for piece in pieces)

        def block(columns):
            return pl.BlockSpec((rows, columns), lambda i: (at // rows, 0))

        outs = (
            shape((rank, every if last else rows), F32),
            *[shape((2 * rank, units), F32)] * 2,
        )
        depth = rest // 2
        return call(
            functools.partial(back_kernel, last, len(pieces)),
            outs,
            24 if last else 44,
            flops=2 * rows * rest * 2 * units,
            moved=2 * rest * (rows + 2 * units),
            grid=(rest // depth,),
            in_specs=piece_specs(pieces, depth)
            + [flat(units, depth, 0)] * 2
            + [flat(rank, depth, 0)]
            + [block(2 * units), block(rank), block(2 * units), block(2 * units), block(rank)]
            + [whole(rank, units)] * 4
            + [whole(*value.shape) for value in before],
            out_specs=tuple(whole(*s.shape) for s in outs),
            scratch_shapes=[pltpu.VMEM((rows, 2 * units), F32), pltpu.VMEM((rows, rank), F32)],
        )(*pieces, down_w, down_p, down_b, back_0, low_0, factor, hidden, low_in, *small, *before)

    far_2, sums_back = tie((far_2, sums_back))
    pieces_2 = (rows_2, *steps_2, *far_2)
    near = back(False, pieces_2[:3], 0)
    sums, grads, for_other = back(True, pieces_2[3:], 3 * slots, *near)

    me = lax.axis_index("seq").astype(jnp.int32).reshape(1)
    share = width // lax.axis_size("seq")
    scalar = pl.BlockSpec(memory_space=pltpu.SMEM)
    chunks = (*pieces_0, *pieces_1, *pieces_2, got_raw)
    tok, cot = call(
        functools.partial(select_kernel, ((5, 5), (5, 1))),
        (pltpu.VMEM((every, 2 * share), BF16),) * 2,
        VMEM_MIB,
        moved=16 * every * share,
        in_specs=[scalar] + [pl.BlockSpec(memory_space=pl.ANY)] * len(chunks),
        out_specs=(pl.BlockSpec(memory_space=pltpu.VMEM),) * 2,
        scratch_shapes=[pltpu.SemaphoreType.DMA((len(chunks),))],
    )(me, *chunks)
    own, other = call(
        functools.partial(product_kernel, rest, capacity),
        (shape((2, rank, share), F32),) * 2,
        16,
        flops=8 * rank * every * share,
        moved=8 * every * share,
        in_specs=[scalar]
        + [pl.BlockSpec(memory_space=pltpu.VMEM)] * 2
        + [whole(rank, every)] * 8,
    )(me, tok, cot, *exchanged(sums), *sums_back)
    return tuple(
        call(
            final_kernel,
            (
                shape((1, rank, share), F32),
                shape((1, rank, units), F32),
                shape((1, rank, units), F32),
                shape((1, rank, share), F32),
            ),
            8,
            moved=24 * rank * share,
        )(own, swap_core(other), grads, swap_core(for_other))
    )


def solution(mesh):
    return jax.shard_map(
        body,
        mesh=mesh,
        in_specs=(
            P(("dp", "seq"), None),
            P(("dp", "seq"), None),
            P(("dp", "seq"), None),
            P(("dp", "seq"), None),
            P("dp", None, "seq"),
            P("dp", None, "seq"),
            P("dp", "seq", None),
            P("dp", None, None),
            P("dp", None, "seq"),
            P("dp", None, "seq"),
            P("dp", None, None),
        ),
        out_specs=(
            P("dp", None, "seq"),
            P("dp", None, "seq"),
            P("dp", None, "seq"),
            P("dp", None, "seq"),
        ),
        check_vma=False,
    )
```
